32 devices in a mesh: gx: 16 (over z, y, core), gz: 2 (over x).
Axes of the slice: x: 2, y: 2, z: 4, core: 2. Of those that a mesh axis runs over, the one named last changes fastest.
Arguments:
- tokens: bfloat16 [4, 64, 16, 768], P(None, 'gx', 'gz'), may hold values from -60 to 60
- cross_qkv: bfloat16 [768, 2304], P(None, 'gx'), may hold values from -16 to 16
- cross_out: bfloat16 [768, 768], P('gx'), may hold values from -0.21875 to 0.21875
- depth_qkv: bfloat16 [768, 2304], P(None, 'gx'), may hold values from -16 to 16
- depth_out: bfloat16 [768, 768], P('gx'), may hold values from -0.21875 to 0.21875
- up_proj: bfloat16 [768, 3072], P(None, 'gz'), may hold values from -0.21875 to 0.21875
- down_proj: bfloat16 [3072, 768], P('gz'), may hold values from -0.109375 to 0.109375
- gains: float32 [3, 768], replicated, may hold values from 0.5 to 1.5
- head_weight: float32 [768], replicated, may hold values from -0.21875 to 0.21875
- head_bias: float32 [1], replicated, may hold values from -1 to 1
Outputs:
- features: bfloat16 [4, 64, 16, 768], P(None, 'gx', 'gz')
- geotime: float32 [4, 64, 16], P(None, 'gx', 'gz')
The draws below stay inside these ranges and needn't reach their ends.
All inputs are finite; a program needn't handle non-finite values.
Results may differ from the reference program's by a relative error of at most 0.013.
Values may be sent and summed in bfloat16 or wider, within the bound.
No kernel may reach another device: no remote copies, remote signals or barrier semaphores. Data moves between devices by JAX's collectives and lax.ppermute only.
A program may use at most 64 MiB of HBM per device.

```python
import math
import jax
import jax.numpy as jnp
from jax import lax

D = 768
HEADS = 12
HDIM = 64
FF = 3072
INL = 4
XL = 64
DP = 16
N_GZ = 2


def draw_tokens(key, part):
    base = jax.random.normal(key, (INL, XL, DP, D), jnp.float32)
    return jnp.clip(base, -60.0, 60.0).astype(jnp.bfloat16)


def projection_draw(key):
    columns = jax.random.normal(key, (D, 3 * D), jnp.float32) / math.sqrt(D)
    return jnp.clip(columns, -16.0, 16.0).astype(jnp.bfloat16)


def draw_cross_qkv(key, part):
    return projection_draw(jax.random.fold_in(key, 31))


def draw_depth_qkv(key, part):
    return projection_draw(jax.random.fold_in(key, 32))


def block_levels(key, shape, pieces, smallest, top_value):
    level, own = 1.0, jax.random.fold_in(key, 6)
    for axis_at, shards_of in pieces:
        steps = jnp.exp(jax.random.uniform(jax.random.fold_in(own, axis_at), (shards_of,), jnp.float32, smallest / len(pieces), top_value / len(pieces)))
        level = level * jnp.repeat(steps, shape[axis_at] // shards_of).reshape([-1 if axis == axis_at else 1 for axis in range(len(shape))])
    return level


def gaussian(stream_key, dims, scale, limit, shards=(), dtype=jnp.bfloat16):
    drawn = scale * jax.random.normal(stream_key, dims, jnp.float32)
    if shards:
        drawn = drawn * block_levels(stream_key, dims, shards, -0.22, 0.18)
    return jnp.clip(drawn, -limit, limit).astype(dtype)


def setup_inputs(seed: int = 0) -> dict:
    arg_keys = jax.random.split(jax.random.key(seed), 11)
    tokens = draw_tokens(jax.random.fold_in(arg_keys[10], 71), 0)
    cross_qkv = draw_cross_qkv(jax.random.fold_in(arg_keys[10], 71), 0)
    cross_out = gaussian(arg_keys[2], (D, D), D ** -0.5, 0.21875, ((0, 16),))
    depth_qkv = draw_depth_qkv(jax.random.fold_in(arg_keys[10], 71), 0)
    depth_out = gaussian(arg_keys[4], (D, D), D ** -0.5, 0.21875, ((0, 16),))
    up_proj = gaussian(arg_keys[5], (D, FF), D ** -0.5, 0.21875, ((1, 2),))
    down_proj = gaussian(arg_keys[6], (FF, D), FF ** -0.5, 0.109375, ((0, 2),))
    gains = jnp.clip(1.0 + 0.1 * jax.random.normal(arg_keys[7], (3, D), jnp.float32), 0.5, 1.5)
    head_weight = gaussian(arg_keys[8], (D,), D ** -0.5, 0.21875, (), jnp.float32)
    head_bias = jnp.clip(jax.random.uniform(arg_keys[9], (1,), jnp.float32, -1.0, 1.0), -1.0, 1.0)
    return {"tokens": tokens, "cross_qkv": cross_qkv, "cross_out": cross_out, "depth_qkv": depth_qkv, "depth_out": depth_out, "up_proj": up_proj, "down_proj": down_proj, "gains": gains, "head_weight": head_weight, "head_bias": head_bias}


log_span = math.log(256.0)

def encodings(inlines, crosslines, depths, cross_start, depth_start, model_width):
    pairs = model_width // 2
    index = jnp.arange(pairs)
    freq = math.pi * jnp.exp(-log_span * index.astype(jnp.float32) / pairs)
    which = index % 3
    inline_pos = jnp.arange(inlines).astype(jnp.float32)[:, None, None, None]
    cross_pos = (cross_start + jnp.arange(crosslines)).astype(jnp.float32)[None, :, None, None]
    depth_pos = (depth_start + jnp.arange(depths)).astype(jnp.float32)[None, None, :, None]
    zeros = jnp.zeros((inlines, crosslines, depths, pairs), jnp.float32)
    position = jnp.where(which == 0, inline_pos + zeros, jnp.where(which == 1, cross_pos + zeros, depth_pos + zeros))
    angle = position * freq
    return jnp.stack([jnp.sin(angle), jnp.cos(angle)], -1).reshape(inlines, crosslines, depths, model_width)

def normalize(stream, gain):
    scale = lax.rsqrt(lax.optimization_barrier(jnp.mean(stream * stream, -1, keepdims=True)) + 1e-05)
    return (stream * scale * gain).astype(jnp.bfloat16)

def attend(queries, keys, values):
    scale = queries.shape[-1] ** (-0.5)
    scores = jnp.einsum('...qe,...ke->...qk', queries.astype(jnp.float32), keys.astype(jnp.float32)) * scale
    scores = scores - lax.optimization_barrier(jnp.max(scores, -1, keepdims=True))
    expo = jnp.exp(scores)
    weights = (expo / lax.optimization_barrier(jnp.sum(expo, -1, keepdims=True))).astype(jnp.bfloat16)
    mixed = jnp.einsum('...qk,...ke->...qe', weights.astype(jnp.float32), values.astype(jnp.float32))
    return mixed.astype(jnp.bfloat16)

def reference(tokens, cross_qkv, cross_out, depth_qkv, depth_out, up_proj, down_proj, gains, head_weight, head_bias):
    count = INL * XL * DP
    stream = (tokens.astype(jnp.float32) + encodings(INL, XL, DP, 0, 0, D)).reshape(count, D)
    normed = normalize(stream, gains[0])
    packed = jnp.dot(normed, cross_qkv, preferred_element_type=jnp.float32).astype(jnp.bfloat16)
    packed = packed.reshape(INL, XL, DP, 3, HEADS, HDIM)
    lined = jnp.transpose(packed, (3, 0, 2, 4, 1, 5)).reshape(3, INL * DP, HEADS, XL, HDIM)
    mixed = lax.map(lambda trio: attend(trio[0], trio[1], trio[2]), (lined[0], lined[1], lined[2]))
    mixed = jnp.transpose(mixed.reshape(INL, DP, HEADS, XL, HDIM), (0, 3, 1, 2, 4)).reshape(count, D)
    stream = stream + jnp.dot(mixed, cross_out, preferred_element_type=jnp.float32)
    normed = normalize(stream, gains[1])
    packed = jnp.dot(normed, depth_qkv, preferred_element_type=jnp.float32).astype(jnp.bfloat16)
    packed = packed.reshape(INL, XL, DP, 3, HEADS, HDIM)
    lined = jnp.transpose(packed, (3, 0, 1, 4, 2, 5))
    mixed = lax.map(lambda trio: attend(trio[0], trio[1], trio[2]), (lined[0], lined[1], lined[2]))
    mixed = jnp.transpose(mixed, (0, 1, 3, 2, 4)).reshape(count, D)
    stream = stream + jnp.dot(mixed, depth_out, preferred_element_type=jnp.float32)
    normed = normalize(stream, gains[2])
    hidden = jax.nn.gelu(jnp.dot(normed, up_proj, preferred_element_type=jnp.float32)).astype(jnp.bfloat16)
    group = FF // N_GZ
    mlp_sum = jnp.zeros((count, D), jnp.float32)
    for member in range(N_GZ):
        partial_sum = jnp.dot(hidden[:, member * group:(member + 1) * group], down_proj[member * group:(member + 1) * group], preferred_element_type=jnp.float32)
        rounded = lax.optimization_barrier(partial_sum.astype(jnp.bfloat16))
        mlp_sum = mlp_sum + rounded.astype(jnp.float32)
    stream = stream + mlp_sum
    features = stream.astype(jnp.bfloat16).reshape(INL, XL, DP, D)
    thickness = jax.nn.softplus(jnp.dot(stream, head_weight, precision=lax.Precision.HIGHEST) + head_bias[0])
    geotime = jnp.cumsum(thickness.reshape(INL, XL, DP), axis=2)
    return (features, geotime)
```

```python
import math

import jax
import jax.numpy as jnp
import numpy as np
from jax import lax
from jax.experimental import pallas as pl
from jax.experimental.pallas import tpu as pltpu
from jax.sharding import PartitionSpec as P

HDIM = 64


log_span = math.log(256.0)


def carried_in(shard, axis, combine, identity):
    peers, position = (lax.axis_size(axis), lax.axis_index(axis))
    everything = lax.all_gather(shard, axis)
    start = jnp.broadcast_to(jnp.asarray(identity, shard.dtype), shard.shape)

    def step(k, before):
        reached = k < position
        new = combine(before, everything[k])
        return jnp.where(reached, new, before)

    return lax.fori_loop(0, peers, step, start)


def encodings(inlines, crosslines, depths, cross_start, depth_start, model_width):
    pairs = model_width // 2
    index = jnp.arange(pairs)
    freq = math.pi * jnp.exp(-log_span * index.astype(jnp.float32) / pairs)
    which = index % 3
    inline_pos = jnp.arange(inlines).astype(jnp.float32)[:, None, None, None]
    cross_pos = (cross_start + jnp.arange(crosslines)).astype(jnp.float32)[None, :, None, None]
    depth_pos = (depth_start + jnp.arange(depths)).astype(jnp.float32)[None, None, :, None]
    zeros = jnp.zeros((inlines, crosslines, depths, pairs), jnp.float32)
    position = jnp.where(
        which == 0, inline_pos + zeros, jnp.where(which == 1, cross_pos + zeros, depth_pos + zeros)
    )
    angle = position * freq
    return jnp.stack([jnp.sin(angle), jnp.cos(angle)], -1).reshape(
        inlines, crosslines, depths, model_width
    )


def normalize(stream, gain):
    scale = lax.rsqrt(jnp.mean(stream * stream, -1, keepdims=True) + 1e-05)
    return (stream * scale * gain).astype(jnp.bfloat16)


def attend(queries, keys, values):
    scale = queries.shape[-1] ** (-0.5)
    scores = (
        jnp.einsum("...qe,...ke->...qk", queries, keys, preferred_element_type=jnp.float32) * scale
    )
    scores = scores - jnp.max(scores, -1, keepdims=True)
    expo = jnp.exp(scores)
    weights = (expo / jnp.sum(expo, -1, keepdims=True)).astype(jnp.bfloat16)
    mixed = jnp.einsum("...qk,...ke->...qe", weights, values, preferred_element_type=jnp.float32)
    return mixed.astype(jnp.bfloat16)


def attend_items(trio):
    return attend(trio[0], trio[1], trio[2])


def general_body(
    tokens,
    cross_qkv,
    cross_out,
    depth_qkv,
    depth_out,
    up_proj,
    down_proj,
    gains,
    head_weight,
    head_bias,
):
    inlines, cross_dev, depth_dev, model_width = tokens.shape
    tok_rows = inlines * cross_dev * depth_dev
    head_count = model_width // HDIM
    cross_group = lax.axis_size("gx")
    encoding = encodings(
        inlines,
        cross_dev,
        depth_dev,
        lax.axis_index("gx") * cross_dev,
        lax.axis_index("gz") * depth_dev,
        model_width,
    )
    stream = (tokens.astype(jnp.float32) + encoding).reshape(tok_rows, model_width)
    normed = normalize(stream, gains[0])
    packed = jnp.dot(
        normed,
        lax.all_gather(cross_qkv, "gx", axis=1, tiled=True),
        preferred_element_type=jnp.float32,
    ).astype(jnp.bfloat16)
    packed = packed.reshape(inlines, cross_dev, depth_dev, 3, head_count, HDIM)
    lined = jnp.transpose(packed, (3, 0, 2, 4, 1, 5))
    per_item = inlines * depth_dev * head_count // cross_group
    lined = lined.reshape(3, cross_group, per_item, cross_dev, HDIM)
    mixed = attend_items(
        (
            lax.all_to_all(lined[0], "gx", split_axis=0, concat_axis=2, tiled=True),
            lax.all_to_all(lined[1], "gx", split_axis=0, concat_axis=2, tiled=True),
            lax.all_to_all(lined[2], "gx", split_axis=0, concat_axis=2, tiled=True),
        )
    )
    mixed = lax.all_to_all(mixed, "gx", split_axis=2, concat_axis=0, tiled=True)
    mixed = jnp.transpose(
        mixed.reshape(inlines, depth_dev, head_count, cross_dev, HDIM), (0, 3, 1, 2, 4)
    ).reshape(tok_rows, model_width)
    columns = mixed
    stream = stream + jnp.dot(
        columns,
        lax.all_gather(cross_out, "gx", axis=0, tiled=True),
        preferred_element_type=jnp.float32,
    )
    normed = normalize(stream, gains[1])
    packed = jnp.dot(
        normed,
        lax.all_gather(depth_qkv, "gx", axis=1, tiled=True),
        preferred_element_type=jnp.float32,
    ).astype(jnp.bfloat16)
    packed = packed.reshape(inlines, cross_dev, depth_dev, 3, head_count, HDIM)
    lined = jnp.transpose(packed, (3, 0, 1, 4, 2, 5))
    all_keys, all_values = (
        lax.all_gather(lined[1], "gz", axis=3, tiled=True),
        lax.all_gather(lined[2], "gz", axis=3, tiled=True),
    )
    mixed = attend(lined[0], all_keys, all_values)
    mixed = jnp.transpose(mixed, (0, 1, 3, 2, 4)).reshape(tok_rows, model_width)
    columns = mixed
    stream = stream + jnp.dot(
        columns,
        lax.all_gather(depth_out, "gx", axis=0, tiled=True),
        preferred_element_type=jnp.float32,
    )
    normed = normalize(stream, gains[2])
    hidden = jax.nn.gelu(
        jnp.dot(
            lax.all_gather(normed, "gz", axis=0, tiled=True),
            up_proj,
            preferred_element_type=jnp.float32,
        )
    ).astype(jnp.bfloat16)
    stream = stream + lax.psum_scatter(
        jnp.dot(hidden, down_proj, preferred_element_type=jnp.float32).astype(jnp.bfloat16),
        "gz",
        scatter_dimension=0,
        tiled=True,
    ).astype(jnp.float32)
    features = stream.astype(jnp.bfloat16).reshape(inlines, cross_dev, depth_dev, model_width)
    thickness = jax.nn.softplus(
        jnp.dot(stream, head_weight, precision=lax.Precision.HIGHEST) + head_bias[0]
    )
    local_time = jnp.cumsum(thickness.reshape(inlines, cross_dev, depth_dev), axis=2)
    line_total = local_time[:, :, -1]
    carried = carried_in(
        line_total, "gz", lambda earlier, later: earlier + later, jnp.zeros_like(line_total)
    )
    geotime = local_time + carried[:, :, None]
    return (features, geotime)


F32 = jnp.float32
BF16 = jnp.bfloat16
VMEM = pl.BlockSpec(memory_space=pltpu.VMEM)
SMEM = pl.BlockSpec(memory_space=pltpu.SMEM)
ANY = pl.BlockSpec(memory_space=pl.ANY)
NT = (((1,), (1,)), ((), ()))
NEG = -1e30


def call(kernel, outs, in_specs, scratch=(), flops=0, nbytes=0, vmem=40):
    return pl.pallas_call(
        kernel,
        out_shape=outs,
        in_specs=in_specs,
        out_specs=jax.tree.map(lambda _: VMEM, outs),
        scratch_shapes=list(scratch),
        compiler_params=pltpu.CompilerParams(vmem_limit_bytes=vmem * 2**20),
        cost_estimate=pl.CostEstimate(flops=flops, bytes_accessed=nbytes, transcendentals=0),
    )


class Plan:
    def __init__(self, inlines, cross_dev, depth_dev, peers):
        self.rows = rows = inlines * cross_dev * depth_dev
        self.lines = inlines * depth_dev // peers
        index = np.arange(rows)
        line = index // (cross_dev * self.lines) * self.lines + index % self.lines
        self.cross = index // self.lines % cross_dev
        self.inline, self.depth = line // depth_dev, line % depth_dev
        natural = (self.inline * cross_dev + self.cross) * depth_dev + self.depth
        self.to_rows = (natural[:, None] == index[None, :]).astype(np.float32)
        self.natural = natural
        column = self.inline * cross_dev + self.cross
        self.same_column = column[:, None] == column[None, :]
        nat_column, nat_depth = index // depth_dev, index % depth_dev
        below = self.depth[:, None] <= nat_depth[None, :]
        on_column = column[:, None] == nat_column[None, :]
        self.cumulative = (on_column & below).astype(np.float32)
        self.carried = on_column.astype(np.float32)
        self.same_line = index[:, None] % self.lines == index[None, :] % self.lines


def rms(stream, gain):
    scale = lax.rsqrt(jnp.mean(stream * stream, -1, keepdims=True) + 1e-05)
    return (stream * scale * gain).astype(BF16)


def as_column(row, eye):
    return jnp.sum(row * eye, axis=1, keepdims=True)


def as_row(column, eye):
    return jnp.sum(column * eye, axis=0, keepdims=True)


def softplus(value):
    return jnp.maximum(value, 0.0) + jnp.log1p(jnp.exp(-jnp.abs(value)))


def encode_kernel(tokens_ref, encoding_ref, to_rows_ref, gain_ref, stream_ref, normed_ref):
    rows = jnp.dot(to_rows_ref[...], tokens_ref[...], preferred_element_type=F32)
    stream = rows + encoding_ref[...]
    stream_ref[...] = stream
    normed_ref[...] = rms(stream, gain_ref[...])


def head_pair(queries, keys, values, bias):
    lane = lax.broadcasted_iota(jnp.int32, queries.shape, 1)
    outs = []
    for head in range(2):
        own = (lane < HDIM) if head == 0 else (lane >= HDIM)
        masked = jnp.where(own, queries, jnp.zeros_like(queries))
        scores = lax.dot_general(masked, keys, NT, preferred_element_type=F32)
        scores = scores * (HDIM**-0.5) + bias
        scores = scores - jnp.max(scores, -1, keepdims=True)
        expo = jnp.exp(scores)
        weights = (expo / jnp.sum(expo, -1, keepdims=True)).astype(BF16)
        outs.append(jnp.dot(weights, values, preferred_element_type=F32))
    return jnp.where(lane < HDIM, outs[0], outs[1]).astype(BF16)


def pieces(start, size, chunk):
    out, at = [], start
    while at < start + size:
        n = min(chunk - at % chunk, start + size - at)
        out.append((at // chunk, at % chunk, at - start, n))
        at += n
    return out


def qkv_copies(weights_ref, held_ref, sems, width, group, chunk, base):
    copies, at = [], 0
    for g in range(width // group):
        of_group = []
        for kind in range(3):
            for block, row, to, n in pieces(kind * width + g * group, group, chunk):
                of_group.append(
                    pltpu.make_async_copy(
                        weights_ref.at[block, pl.ds(base + row, n), :],
                        held_ref.at[g, kind, pl.ds(to, n), :],
                        sems.at[at],
                    )
                )
                at += 1
        copies.append(of_group)
    return copies


def qkv_copy_count(width, group, chunk):
    return sum(
        len(pieces(kind * width + g * group, group, chunk))
        for g in range(width // group)
        for kind in range(3)
    )


def cross_kernel(normed_ref, weights_ref, bias_ref, mixed_ref, held_ref, sems):
    width, group = normed_ref.shape[1], held_ref.shape[2]
    copies = qkv_copies(weights_ref, held_ref, sems, width, group, weights_ref.shape[1], 0)
    for of_group in copies:
        for copy in of_group:
            copy.start()
    bias = bias_ref[...]
    for g, of_group in enumerate(copies):
        for copy in of_group:
            copy.wait()
        normed = normed_ref[...]
        q, k, v = (
            lax.dot_general(normed, held_ref[g, kind], NT, preferred_element_type=F32).astype(BF16)
            for kind in range(3)
        )
        for pair in range(group // 128):
            at = slice(pair * 128, pair * 128 + 128)
            mixed_ref[:, g * group + pair * 128 : g * group + pair * 128 + 128] = head_pair(
                q[:, at], k[:, at], v[:, at], bias
            )


def row_copies(weights_ref, held_ref, sems, base, count):
    return [
        pltpu.make_async_copy(
            weights_ref.at[block, pl.ds(base, count), :],
            held_ref.at[pl.ds(block * count, count), :],
            sems.at[block],
        )
        for block in range(weights_ref.shape[0])
    ]


def cross_out_kernel(
    mixed_ref, stream_ref, weights_ref, gain_ref, out_ref, normed_ref, held_ref, sems, *, base, count
):
    copies = row_copies(weights_ref, held_ref, sems, base, count)
    for copy in copies:
        copy.start()
    for copy in copies:
        copy.wait()
    stream = stream_ref[...] + jnp.dot(mixed_ref[...], held_ref[...], preferred_element_type=F32)
    out_ref[...] = stream
    normed_ref[...] = rms(stream, gain_ref[...])


def depth_kernel(
    own_ref,
    peer_ref,
    stream_ref,
    weights_ref,
    bias_ref,
    gain_ref,
    out_ref,
    normed_ref,
    held_ref,
    out_held_ref,
    sems,
    out_sems,
    *,
    chunk,
    base,
    count,
):
    width, group = own_ref.shape[1], held_ref.shape[2]
    copies = qkv_copies(weights_ref, held_ref, sems, width, group, chunk, 0)
    out_copies = row_copies(weights_ref, out_held_ref, out_sems, base, count)
    for of_group in copies:
        for copy in of_group:
            copy.start()
    for copy in out_copies:
        copy.start()
    bias = bias_ref[...]
    mixed = []
    for g, of_group in enumerate(copies):
        for copy in of_group:
            copy.wait()
        own = own_ref[...]
        both = jnp.concatenate([own, peer_ref[...]], axis=0)
        q = lax.dot_general(own, held_ref[g, 0], NT, preferred_element_type=F32).astype(BF16)
        k, v = (
            lax.dot_general(both, held_ref[g, kind], NT, preferred_element_type=F32).astype(BF16)
            for kind in (1, 2)
        )
        for pair in range(group // 128):
            at = slice(pair * 128, pair * 128 + 128)
            mixed.append(head_pair(q[:, at], k[:, at], v[:, at], bias))
    for copy in out_copies:
        copy.wait()
    stream = stream_ref[...] + jnp.dot(
        jnp.concatenate(mixed, axis=1), out_held_ref[...], preferred_element_type=F32
    )
    out_ref[...] = stream
    normed_ref[...] = rms(stream, gain_ref[...])


def mlp_kernel(
    own_ref, peer_ref, stream_ref, up_ref, down_ref, head_ref, eye_ref,
    own_part_ref, peer_part_ref, own_head_ref, peer_head_ref,
):
    rows = own_ref.shape[0]
    both = jnp.concatenate([own_ref[...], peer_ref[...]], axis=0)
    hidden = jnp.dot(both, up_ref[...], preferred_element_type=F32)
    hidden = jax.nn.gelu(hidden).astype(BF16)
    part = jnp.dot(hidden, down_ref[...], preferred_element_type=F32).astype(BF16)
    own_part_ref[...] = part[:rows]
    peer_part_ref[...] = part[rows:]
    head, eye = head_ref[...], eye_ref[...]
    own = jnp.sum((stream_ref[...] + part[:rows].astype(F32)) * head, axis=1, keepdims=True)
    peer = jnp.sum(part[rows:].astype(F32) * head, axis=1, keepdims=True)
    own_head_ref[...] = as_row(own, eye)
    peer_head_ref[...] = as_row(peer, eye)


def final_kernel(
    stream_ref, own_ref, got_ref, own_head_ref, got_head_ref, peer_head_ref,
    head_ref, bias_ref, later_ref, from_rows_ref, eye_ref, cumulative_ref, carried_ref,
    features_ref, time_ref,
):
    got = got_ref[...].astype(F32)
    stream = stream_ref[...] + own_ref[...].astype(F32) + got
    features_ref[...] = jnp.dot(
        from_rows_ref[...], stream.astype(BF16), preferred_element_type=F32
    ).astype(BF16)
    eye = eye_ref[...]
    bias = bias_ref[0]
    own = as_column(own_head_ref[...], eye) + jnp.sum(got * head_ref[...], axis=1, keepdims=True)
    own = softplus(own + bias)
    before = softplus(as_column(got_head_ref[...] + peer_head_ref[...], eye) + bias) * later_ref[0]
    time_ref[...] = jnp.sum(
        own * cumulative_ref[...] + before * carried_ref[...], axis=0, keepdims=True
    )


def fast_body(
    tokens, cross_qkv, cross_out, depth_qkv, depth_out,
    up_proj, down_proj, gains, head_weight, head_bias,
):
    inlines, cross_dev, depth_dev, width = tokens.shape
    peers = lax.axis_size("gx")
    plan = Plan(inlines, cross_dev, depth_dev, peers)
    rows, group = plan.rows, 256
    chunk, count = cross_qkv.shape[1], cross_out.shape[0]
    swap = [(0, 1), (1, 0)]
    def const(a, dtype=F32):
        return jnp.asarray(np.asarray(a, np.float32), dtype)
    eye = const(np.eye(rows))

    cross_w = lax.all_gather(cross_qkv.T, "gx", axis=0)
    rest = jnp.concatenate([depth_qkv.T, cross_out, depth_out], axis=0)
    rest_w = lax.all_gather(rest, "gx", axis=0)

    with jax.named_scope("encoding"):
        pairs = width // 2
        feature = jnp.arange(width)
        pair = feature // 2
        freq = math.pi * jnp.exp(-log_span * pair.astype(F32) / pairs)
        which = pair % 3
        at_cross = const(plan.cross) + (lax.axis_index("gx") * cross_dev).astype(F32)
        at_depth = const(plan.depth) + (lax.axis_index("gz") * depth_dev).astype(F32)
        position = jnp.where(
            which == 0,
            const(plan.inline)[:, None],
            jnp.where(which == 1, at_cross[:, None], at_depth[:, None]),
        )
        angle = position * freq
        encoding = jnp.where(feature % 2 == 0, jnp.sin(angle), jnp.cos(angle))

    shape = jax.ShapeDtypeStruct
    wide, narrow = shape((rows, width), F32), shape((rows, width), BF16)
    row = shape((1, rows), F32)
    stream, normed = call(encode_kernel, (wide, narrow), [VMEM] * 4)(
        tokens.reshape(rows, width), encoding, const(plan.to_rows, BF16), gains[0:1]
    )
    lined = lax.all_to_all(
        normed.reshape(peers, rows // peers, width), "gx", split_axis=0, concat_axis=0, tiled=True
    )
    n_copies = qkv_copy_count(width, group, chunk)
    held = pltpu.VMEM((width // group, 3, group, width), BF16)
    mixed = call(
        cross_kernel,
        narrow,
        [VMEM, ANY, VMEM],
        [held, pltpu.SemaphoreType.DMA((n_copies,))],
    )(lined.reshape(rows, width), cross_w, const(np.where(plan.same_line, 0.0, NEG)))
    mixed = lax.all_to_all(
        mixed.reshape(peers, rows // peers, width), "gx", split_axis=0, concat_axis=0, tiled=True
    )
    out_held = pltpu.VMEM((width, width), BF16)

    def cross_out_step(*refs):
        cross_out_kernel(*refs, base=chunk, count=count)

    stream, normed = call(
        cross_out_step,
        (wide, narrow),
        [VMEM, VMEM, ANY, VMEM],
        [out_held, pltpu.SemaphoreType.DMA((peers,))],
    )(mixed.reshape(rows, width), stream, rest_w, gains[1:2])
    peer = lax.ppermute(normed, "gz", swap)

    def depth_step(*refs):
        depth_kernel(*refs, chunk=chunk, base=chunk + count, count=count)

    depth_bias = np.where(plan.same_column, 0.0, NEG)
    stream, normed = call(
        depth_step,
        (wide, narrow),
        [VMEM, VMEM, VMEM, ANY, VMEM, VMEM],
        [held, out_held, pltpu.SemaphoreType.DMA((n_copies,)), pltpu.SemaphoreType.DMA((peers,))],
    )(
        normed, peer, stream, rest_w,
        const(np.concatenate([depth_bias, depth_bias], axis=1)), gains[2:3],
    )
    peer = lax.ppermute(normed, "gz", swap)
    head = head_weight.reshape(1, width)
    own_part, peer_part, own_head, peer_head = call(
        mlp_kernel, (narrow, narrow, row, row), [VMEM] * 7
    )(normed, peer, stream, up_proj, down_proj, head, eye)
    got_part = lax.ppermute(peer_part, "gz", swap)
    got_head = lax.ppermute(own_head, "gz", swap)
    later = (lax.axis_index("gz") > 0).astype(F32).reshape(1)
    features, geotime = call(
        final_kernel, (narrow, row), [VMEM] * 7 + [SMEM, SMEM] + [VMEM] * 4
    )(
        stream, own_part, got_part, own_head, got_head, peer_head,
        head, head_bias, later, const(plan.to_rows.T, BF16), eye,
        const(plan.cumulative), const(plan.carried),
    )
    return features.reshape(tokens.shape), geotime.reshape(tokens.shape[:3])


def solution(mesh):
    def body(*args):
        tokens = args[0]
        inlines, cross_dev, depth_dev, width = tokens.shape
        peers = mesh.shape["gx"]
        fits = (
            mesh.shape["gz"] == 2
            and inlines * depth_dev % peers == 0
            and inlines * cross_dev * depth_dev == 128
            and width % 256 == 0
            and 3 * width % (16 * peers) == 0
            and width % (16 * peers) == 0
        )
        return (fast_body if fits else general_body)(*args)

    return jax.shard_map(
        body,
        mesh=mesh,
        in_specs=(
            P(None, "gx", "gz", None),
            P(None, "gx"),
            P("gx", None),
            P(None, "gx"),
            P("gx", None),
            P(None, "gz"),
            P("gz", None),
            P(),
            P(),
            P(),
        ),
        out_specs=(P(None, "gx", "gz", None), P(None, "gx", "gz")),
        check_vma=False,
    )
```

```python
import math

import jax
import jax.numpy as jnp
import numpy as np
from jax import lax
from jax.experimental import pallas as pl
from jax.experimental.pallas import tpu as pltpu
from jax.sharding import PartitionSpec as P

HDIM = 64


log_span = math.log(256.0)


def carried_in(shard, axis, combine, identity):
    peers, position = (lax.axis_size(axis), lax.axis_index(axis))
    everything = lax.all_gather(shard, axis)
    start = jnp.broadcast_to(jnp.asarray(identity, shard.dtype), shard.shape)

    def step(k, before):
        reached = k < position
        new = combine(before, everything[k])
        return jnp.where(reached, new, before)

    return lax.fori_loop(0, peers, step, start)


def encodings(inlines, crosslines, depths, cross_start, depth_start, model_width):
    pairs = model_width // 2
    index = jnp.arange(pairs)
    freq = math.pi * jnp.exp(-log_span * index.astype(jnp.float32) / pairs)
    which = index % 3
    inline_pos = jnp.arange(inlines).astype(jnp.float32)[:, None, None, None]
    cross_pos = (cross_start + jnp.arange(crosslines)).astype(jnp.float32)[None, :, None, None]
    depth_pos = (depth_start + jnp.arange(depths)).astype(jnp.float32)[None, None, :, None]
    zeros = jnp.zeros((inlines, crosslines, depths, pairs), jnp.float32)
    position = jnp.where(
        which == 0, inline_pos + zeros, jnp.where(which == 1, cross_pos + zeros, depth_pos + zeros)
    )
    angle = position * freq
    return jnp.stack([jnp.sin(angle), jnp.cos(angle)], -1).reshape(
        inlines, crosslines, depths, model_width
    )


def normalize(stream, gain):
    scale = lax.rsqrt(jnp.mean(stream * stream, -1, keepdims=True) + 1e-05)
    return (stream * scale * gain).astype(jnp.bfloat16)


def attend(queries, keys, values):
    scale = queries.shape[-1] ** (-0.5)
    scores = (
        jnp.einsum("...qe,...ke->...qk", queries, keys, preferred_element_type=jnp.float32) * scale
    )
    scores = scores - jnp.max(scores, -1, keepdims=True)
    expo = jnp.exp(scores)
    weights = (expo / jnp.sum(expo, -1, keepdims=True)).astype(jnp.bfloat16)
    mixed = jnp.einsum("...qk,...ke->...qe", weights, values, preferred_element_type=jnp.float32)
    return mixed.astype(jnp.bfloat16)


def attend_items(trio):
    return attend(trio[0], trio[1], trio[2])


def general_body(
    tokens,
    cross_qkv,
    cross_out,
    depth_qkv,
    depth_out,
    up_proj,
    down_proj,
    gains,
    head_weight,
    head_bias,
):
    inlines, cross_dev, depth_dev, model_width = tokens.shape
    tok_rows = inlines * cross_dev * depth_dev
    head_count = model_width // HDIM
    cross_group = lax.axis_size("gx")
    encoding = encodings(
        inlines,
        cross_dev,
        depth_dev,
        lax.axis_index("gx") * cross_dev,
        lax.axis_index("gz") * depth_dev,
        model_width,
    )
    stream = (tokens.astype(jnp.float32) + encoding).reshape(tok_rows, model_width)
    normed = normalize(stream, gains[0])
    packed = jnp.dot(
        normed,
        lax.all_gather(cross_qkv, "gx", axis=1, tiled=True),
        preferred_element_type=jnp.float32,
    ).astype(jnp.bfloat16)
    packed = packed.reshape(inlines, cross_dev, depth_dev, 3, head_count, HDIM)
    lined = jnp.transpose(packed, (3, 0, 2, 4, 1, 5))
    per_item = inlines * depth_dev * head_count // cross_group
    lined = lined.reshape(3, cross_group, per_item, cross_dev, HDIM)
    mixed = attend_items(
        (
            lax.all_to_all(lined[0], "gx", split_axis=0, concat_axis=2, tiled=True),
            lax.all_to_all(lined[1], "gx", split_axis=0, concat_axis=2, tiled=True),
            lax.all_to_all(lined[2], "gx", split_axis=0, concat_axis=2, tiled=True),
        )
    )
    mixed = lax.all_to_all(mixed, "gx", split_axis=2, concat_axis=0, tiled=True)
    mixed = jnp.transpose(
        mixed.reshape(inlines, depth_dev, head_count, cross_dev, HDIM), (0, 3, 1, 2, 4)
    ).reshape(tok_rows, model_width)
    columns = mixed
    stream = stream + jnp.dot(
        columns,
        lax.all_gather(cross_out, "gx", axis=0, tiled=True),
        preferred_element_type=jnp.float32,
    )
    normed = normalize(stream, gains[1])
    packed = jnp.dot(
        normed,
        lax.all_gather(depth_qkv, "gx", axis=1, tiled=True),
        preferred_element_type=jnp.float32,
    ).astype(jnp.bfloat16)
    packed = packed.reshape(inlines, cross_dev, depth_dev, 3, head_count, HDIM)
    lined = jnp.transpose(packed, (3, 0, 1, 4, 2, 5))
    all_keys, all_values = (
        lax.all_gather(lined[1], "gz", axis=3, tiled=True),
        lax.all_gather(lined[2], "gz", axis=3, tiled=True),
    )
    mixed = attend(lined[0], all_keys, all_values)
    mixed = jnp.transpose(mixed, (0, 1, 3, 2, 4)).reshape(tok_rows, model_width)
    columns = mixed
    stream = stream + jnp.dot(
        columns,
        lax.all_gather(depth_out, "gx", axis=0, tiled=True),
        preferred_element_type=jnp.float32,
    )
    normed = normalize(stream, gains[2])
    hidden = jax.nn.gelu(
        jnp.dot(
            lax.all_gather(normed, "gz", axis=0, tiled=True),
            up_proj,
            preferred_element_type=jnp.float32,
        )
    ).astype(jnp.bfloat16)
    stream = stream + lax.psum_scatter(
        jnp.dot(hidden, down_proj, preferred_element_type=jnp.float32).astype(jnp.bfloat16),
        "gz",
        scatter_dimension=0,
        tiled=True,
    ).astype(jnp.float32)
    features = stream.astype(jnp.bfloat16).reshape(inlines, cross_dev, depth_dev, model_width)
    thickness = jax.nn.softplus(
        jnp.dot(stream, head_weight, precision=lax.Precision.HIGHEST) + head_bias[0]
    )
    local_time = jnp.cumsum(thickness.reshape(inlines, cross_dev, depth_dev), axis=2)
    line_total = local_time[:, :, -1]
    carried = carried_in(
        line_total, "gz", lambda earlier, later: earlier + later, jnp.zeros_like(line_total)
    )
    geotime = local_time + carried[:, :, None]
    return (features, geotime)


F32 = jnp.float32
BF16 = jnp.bfloat16
VMEM = pl.BlockSpec(memory_space=pltpu.VMEM)
SMEM = pl.BlockSpec(memory_space=pltpu.SMEM)
HBM = pl.BlockSpec(memory_space=pltpu.HBM)
NT = (((1,), (1,)), ((), ()))
NEG = -1e30


def call(kernel, outs, in_specs, scratch=(), flops=0, nbytes=0, vmem=40):
    return pl.pallas_call(
        kernel,
        out_shape=outs,
        in_specs=in_specs,
        out_specs=jax.tree.map(lambda _: VMEM, outs),
        scratch_shapes=list(scratch),
        compiler_params=pltpu.CompilerParams(vmem_limit_bytes=vmem * 2**20),
        cost_estimate=pl.CostEstimate(flops=flops, bytes_accessed=nbytes, transcendentals=0),
    )


class Plan:
    def __init__(self, inlines, cross_dev, depth_dev, peers):
        self.rows = rows = inlines * cross_dev * depth_dev
        self.lines = inlines * depth_dev // peers
        index = np.arange(rows)
        line = index // (cross_dev * self.lines) * self.lines + index % self.lines
        self.cross = index // self.lines % cross_dev
        self.inline, self.depth = line // depth_dev, line % depth_dev
        natural = (self.inline * cross_dev + self.cross) * depth_dev + self.depth
        self.to_rows = (natural[:, None] == index[None, :]).astype(np.float32)
        self.natural = natural
        column = self.inline * cross_dev + self.cross
        self.same_column = column[:, None] == column[None, :]
        nat_column, nat_depth = index // depth_dev, index % depth_dev
        below = self.depth[:, None] <= nat_depth[None, :]
        on_column = column[:, None] == nat_column[None, :]
        self.cumulative = (on_column & below).astype(np.float32)
        self.carried = on_column.astype(np.float32)
        self.same_line = index[:, None] % self.lines == index[None, :] % self.lines


def rms(stream, gain):
    scale = lax.rsqrt(jnp.mean(stream * stream, -1, keepdims=True) + 1e-05)
    return (stream * scale * gain).astype(BF16)


def as_column(row, eye):
    return jnp.sum(row * eye, axis=1, keepdims=True)


def as_row(column, eye):
    return jnp.sum(column * eye, axis=0, keepdims=True)


def softplus(value):
    return jnp.maximum(value, 0.0) + jnp.log1p(jnp.exp(-jnp.abs(value)))


def encode_kernel(tokens_ref, encoding_ref, to_rows_ref, gain_ref, stream_ref, normed_ref):
    rows = jnp.dot(to_rows_ref[...], tokens_ref[...], preferred_element_type=F32)
    stream = rows + encoding_ref[...]
    stream_ref[...] = stream
    normed_ref[...] = rms(stream, gain_ref[...])


def attend_heads(queries, keys, values, bias):
    lane = lax.broadcasted_iota(jnp.int32, (queries.shape[0], 128), 1)
    ones = jnp.ones((keys.shape[0], 128), BF16)
    outs = []
    for at in range(0, queries.shape[1], 128):
        at = slice(at, at + 128)
        wide = jnp.concatenate([values[:, at], ones], axis=1)
        pair = []
        for own in (lane < HDIM, lane >= HDIM):
            masked = jnp.where(own, queries[:, at], jnp.zeros_like(queries[:, at]))
            scores = lax.dot_general(masked, keys[:, at], NT, preferred_element_type=F32) + bias
            expo = jnp.exp(scores - jnp.max(scores, -1, keepdims=True)).astype(BF16)
            mixed = jnp.dot(expo, wide, preferred_element_type=F32)
            pair.append(mixed[:, :128] / mixed[:, 128:])
        outs.append(jnp.where(lane < HDIM, pair[0], pair[1]).astype(BF16))
    return jnp.concatenate(outs, axis=1)


def project(normed, weights):
    return lax.dot_general(normed, weights, NT, preferred_element_type=F32).astype(BF16)


def cross_kernel(*refs, places):
    position_ref, normed_ref, bias_ref = refs[:3]
    piece_refs, (mixed_ref, held_ref) = refs[3:-2], refs[-2:]
    width = normed_ref.shape[1]
    y, c, x = position_ref[0], position_ref[1], position_ref[2]
    for piece_ref, (first, other_y, other_c, other_x) in zip(piece_refs, places):
        planes, rows, lanes = piece_ref.shape
        at_y = 1 - y if other_y else y
        at_c = 1 - c if other_c else c
        at_x = 1 - x if other_x else x
        at_lane = pl.multiple_of(at_x * lanes, 128)
        for plane in range(planes):
            block = (first + plane) * 4 + at_y * 2 + at_c
            at_row = pl.multiple_of(block * rows, 16)
            held_ref[pl.ds(at_row, rows), pl.ds(at_lane, lanes)] = piece_ref[plane]
    normed = normed_ref[...]
    q = project(normed, held_ref[:width]) * BF16(HDIM**-0.5)
    k = project(normed, held_ref[width : 2 * width])
    v = project(normed, held_ref[2 * width :])
    mixed_ref[...] = attend_heads(q, k, v, bias_ref[...])


def chunk_copy(weights_ref, held_ref, sem, base, count):
    return pltpu.make_async_copy(weights_ref.at[:, pl.ds(base, count), :], held_ref, sem)


def flat(ref):
    held = ref[...]
    return held.reshape(held.shape[0] * held.shape[1], held.shape[2])


def cross_out_kernel(
    mixed_ref, stream_ref, weights_ref, gain_ref, out_ref, normed_ref, held_ref, sem, *, base, count
):
    copy = chunk_copy(weights_ref, held_ref, sem, base, count)
    copy.start()
    copy.wait()
    stream = stream_ref[...] + jnp.dot(mixed_ref[...], flat(held_ref), preferred_element_type=F32)
    out_ref[...] = stream
    normed_ref[...] = rms(stream, gain_ref[...])


def depth_kernel(
    own_ref, peer_ref, stream_ref, weights_ref, bias_ref, gain_ref,
    out_ref, normed_ref, held_ref, out_held_ref, sem, out_sem, *, chunk, base, count,
):
    width = own_ref.shape[1]
    copy = chunk_copy(weights_ref, held_ref, sem, 0, chunk)
    out_copy = chunk_copy(weights_ref, out_held_ref, out_sem, base, count)
    copy.start()
    out_copy.start()
    own = own_ref[...]
    both = jnp.concatenate([own, peer_ref[...]], axis=0)
    copy.wait()
    weights = flat(held_ref)
    q = project(own, weights[:width]) * BF16(HDIM**-0.5)
    k = project(both, weights[width : 2 * width])
    v = project(both, weights[2 * width :])
    mixed = attend_heads(q, k, v, bias_ref[...])
    out_copy.wait()
    stream = stream_ref[...] + jnp.dot(mixed, flat(out_held_ref), preferred_element_type=F32)
    out_ref[...] = stream
    normed_ref[...] = rms(stream, gain_ref[...])


def gather_planes(shard, peers):
    lanes = shard.shape[1] // 2
    half = lax.dynamic_slice_in_dim(shard, lax.axis_index("gz") * lanes, lanes, axis=1)
    planes = peers // 4
    groups = [[4 * z + k for z in range(planes)] for k in range(4)]
    own = lax.all_gather(half, "gx", axis=0, axis_index_groups=groups)

    def to_x(a):
        return lax.ppermute(a, "gz", [(0, 1), (1, 0)])

    def to_y(a):
        return lax.ppermute(a, "gx", [(i, i ^ 2) for i in range(peers)])

    def to_core(a):
        return lax.ppermute(a, "gx", [(i, i ^ 1) for i in range(peers)])

    low, high = own[: planes // 2], own[planes // 2 :]
    at = planes // 2
    low_x, high_y, low_y, high_x = to_x(low), to_y(high), to_y(low), to_x(high)
    low_xy, high_xy = to_y(low_x), to_x(high_y)
    pieces = [own, low_x, high_y, low_y, high_x, low_xy, high_xy]
    places = [(0, 0, 0), (0, 0, 1), (at, 1, 0), (0, 1, 0), (at, 0, 1), (0, 1, 1), (at, 1, 1)]
    both = [(f, y, 0, x) for f, y, x in places] + [(f, y, 1, x) for f, y, x in places]
    return pieces + [to_core(piece) for piece in pieces], both


def mlp_kernel(
    own_ref, peer_ref, stream_ref, up_ref, down_ref, head_ref, eye_ref,
    own_part_ref, peer_part_ref, own_head_ref, peer_head_ref,
):
    rows = own_ref.shape[0]
    both = jnp.concatenate([own_ref[...], peer_ref[...]], axis=0)
    hidden = jnp.dot(both, up_ref[...], preferred_element_type=F32)
    hidden = jax.nn.gelu(hidden).astype(BF16)
    part = jnp.dot(hidden, down_ref[...], preferred_element_type=F32).astype(BF16)
    own_part_ref[...] = part[:rows]
    peer_part_ref[...] = part[rows:]
    head, eye = head_ref[...], eye_ref[...]
    own = jnp.sum((stream_ref[...] + part[:rows].astype(F32)) * head, axis=1, keepdims=True)
    peer = jnp.sum(part[rows:].astype(F32) * head, axis=1, keepdims=True)
    own_head_ref[...] = as_row(own, eye)
    peer_head_ref[...] = as_row(peer, eye)


def final_kernel(
    stream_ref, own_ref, got_ref, own_head_ref, got_head_ref, peer_head_ref,
    head_ref, bias_ref, later_ref, from_rows_ref, eye_ref, cumulative_ref, carried_ref,
    features_ref, time_ref,
):
    got = got_ref[...].astype(F32)
    stream = stream_ref[...] + own_ref[...].astype(F32) + got
    features_ref[...] = jnp.dot(
        from_rows_ref[...], stream.astype(BF16), preferred_element_type=F32
    ).astype(BF16)
    eye = eye_ref[...]
    bias = bias_ref[0]
    own = as_column(own_head_ref[...], eye) + jnp.sum(got * head_ref[...], axis=1, keepdims=True)
    own = softplus(own + bias)
    before = softplus(as_column(got_head_ref[...] + peer_head_ref[...], eye) + bias) * later_ref[0]
    time_ref[...] = jnp.sum(
        own * cumulative_ref[...] + before * carried_ref[...], axis=0, keepdims=True
    )


def fast_body(
    tokens, cross_qkv, cross_out, depth_qkv, depth_out,
    up_proj, down_proj, gains, head_weight, head_bias,
):
    inlines, cross_dev, depth_dev, width = tokens.shape
    peers = lax.axis_size("gx")
    plan = Plan(inlines, cross_dev, depth_dev, peers)
    rows = plan.rows
    chunk, count = cross_qkv.shape[1], cross_out.shape[0]
    swap = [(0, 1), (1, 0)]
    def const(a, dtype=F32):
        return jnp.asarray(np.asarray(a, np.float32), dtype)
    eye = const(np.eye(rows))

    rest = jnp.concatenate([depth_qkv.T, cross_out, depth_out], axis=0)
    rest_w = lax.all_gather(rest, "gx", axis=0)
    cross_pieces, places = gather_planes(cross_qkv.T, peers)
    gx = lax.axis_index("gx")
    place = jnp.stack([gx // 2 % 2, gx % 2, lax.axis_index("gz")]).astype(jnp.int32)

    with jax.named_scope("encoding"):
        pairs = width // 2
        feature = jnp.arange(width)
        pair = feature // 2
        freq = math.pi * jnp.exp(-log_span * pair.astype(F32) / pairs)
        which = pair % 3
        at_cross = const(plan.cross) + (lax.axis_index("gx") * cross_dev).astype(F32)
        at_depth = const(plan.depth) + (lax.axis_index("gz") * depth_dev).astype(F32)
        position = jnp.where(
            which == 0,
            const(plan.inline)[:, None],
            jnp.where(which == 1, at_cross[:, None], at_depth[:, None]),
        )
        angle = position * freq
        encoding = jnp.where(feature % 2 == 0, jnp.sin(angle), jnp.cos(angle))

    shape = jax.ShapeDtypeStruct
    wide, narrow = shape((rows, width), F32), shape((rows, width), BF16)
    row = shape((1, rows), F32)
    stream, normed = call(encode_kernel, (wide, narrow), [VMEM] * 4)(
        tokens.reshape(rows, width), encoding, const(plan.to_rows, BF16), gains[0:1]
    )
    lined = lax.all_to_all(
        normed.reshape(peers, rows // peers, width), "gx", split_axis=0, concat_axis=0, tiled=True
    )

    def cross_step(*refs):
        cross_kernel(*refs, places=places)

    mixed = call(
        cross_step,
        narrow,
        [SMEM] + [VMEM] * (2 + len(cross_pieces)),
        [pltpu.VMEM((3 * width, width), BF16)],
    )(
        place, lined.reshape(rows, width), const(np.where(plan.same_line, 0.0, NEG)), *cross_pieces
    )
    mixed = lax.all_to_all(
        mixed.reshape(peers, rows // peers, width), "gx", split_axis=0, concat_axis=0, tiled=True
    )
    out_held = pltpu.VMEM((peers, count, width), BF16)
    held = pltpu.VMEM((peers, chunk, width), BF16)

    def cross_out_step(*refs):
        cross_out_kernel(*refs, base=chunk, count=count)

    stream, normed = call(
        cross_out_step,
        (wide, narrow),
        [VMEM, VMEM, HBM, VMEM],
        [out_held, pltpu.SemaphoreType.DMA],
    )(mixed.reshape(rows, width), stream, rest_w, gains[1:2])
    peer = lax.ppermute(normed, "gz", swap)

    def depth_step(*refs):
        depth_kernel(*refs, chunk=chunk, base=chunk + count, count=count)

    depth_bias = np.where(plan.same_column, 0.0, NEG)
    stream, normed = call(
        depth_step,
        (wide, narrow),
        [VMEM, VMEM, VMEM, HBM, VMEM, VMEM],
        [held, out_held, pltpu.SemaphoreType.DMA, pltpu.SemaphoreType.DMA],
    )(
        normed, peer, stream, rest_w,
        const(np.concatenate([depth_bias, depth_bias], axis=1)), gains[2:3],
    )
    peer = lax.ppermute(normed, "gz", swap)
    head = head_weight.reshape(1, width)
    own_part, peer_part, own_head, peer_head = call(
        mlp_kernel, (narrow, narrow, row, row), [VMEM] * 7
    )(normed, peer, stream, up_proj, down_proj, head, eye)
    got_part = lax.ppermute(peer_part, "gz", swap)
    got_head = lax.ppermute(own_head, "gz", swap)
    later = (lax.axis_index("gz") > 0).astype(F32).reshape(1)
    features, geotime = call(
        final_kernel, (narrow, row), [VMEM] * 7 + [SMEM, SMEM] + [VMEM] * 4
    )(
        stream, own_part, got_part, own_head, got_head, peer_head,
        head, head_bias, later, const(plan.to_rows.T, BF16), eye,
        const(plan.cumulative), const(plan.carried),
    )
    return features.reshape(tokens.shape), geotime.reshape(tokens.shape[:3])


def solution(mesh):
    def body(*args):
        tokens = args[0]
        inlines, cross_dev, depth_dev, width = tokens.shape
        peers = mesh.shape["gx"]
        fits = (
            mesh.shape["gz"] == 2
            and inlines * depth_dev % peers == 0
            and inlines * cross_dev * depth_dev == 128
            and width % 256 == 0
            and peers == 16
            and 3 * width % (16 * peers) == 0
            and width % (16 * peers) == 0
        )
        return (fast_body if fits else general_body)(*args)

    return jax.shard_map(
        body,
        mesh=mesh,
        in_specs=(
            P(None, "gx", "gz", None),
            P(None, "gx"),
            P("gx", None),
            P(None, "gx"),
            P("gx", None),
            P(None, "gz"),
            P("gz", None),
            P(),
            P(),
            P(),
        ),
        out_specs=(P(None, "gx", "gz", None), P(None, "gx", "gz")),
        check_vma=False,
    )
```

```python
import math
import functools

import jax
import jax.numpy as jnp
from jax import lax
from jax.experimental import pallas as pl
from jax.experimental.pallas import tpu as pltpu
from jax.sharding import PartitionSpec as P

HDIM = 64


log_span = math.log(256.0)


def carried_in(shard, axis, combine, identity):
    peers, position = (lax.axis_size(axis), lax.axis_index(axis))
    everything = lax.all_gather(shard, axis)
    start = jnp.broadcast_to(jnp.asarray(identity, shard.dtype), shard.shape)

    def step(k, before):
        reached = k < position
        new = combine(before, everything[k])
        return jnp.where(reached, new, before)

    return lax.fori_loop(0, peers, step, start)


def encodings(inlines, crosslines, depths, cross_start, depth_start, model_width):
    pairs = model_width // 2
    index = jnp.arange(pairs)
    freq = math.pi * jnp.exp(-log_span * index.astype(jnp.float32) / pairs)
    which = index % 3
    inline_pos = jnp.arange(inlines).astype(jnp.float32)[:, None, None, None]
    cross_pos = (cross_start + jnp.arange(crosslines)).astype(jnp.float32)[None, :, None, None]
    depth_pos = (depth_start + jnp.arange(depths)).astype(jnp.float32)[None, None, :, None]
    zeros = jnp.zeros((inlines, crosslines, depths, pairs), jnp.float32)
    position = jnp.where(
        which == 0, inline_pos + zeros, jnp.where(which == 1, cross_pos + zeros, depth_pos + zeros)
    )
    angle = position * freq
    return jnp.stack([jnp.sin(angle), jnp.cos(angle)], -1).reshape(
        inlines, crosslines, depths, model_width
    )


def normalize(stream, gain):
    scale = lax.rsqrt(jnp.mean(stream * stream, -1, keepdims=True) + 1e-05)
    return (stream * scale * gain).astype(jnp.bfloat16)


def attend(queries, keys, values):
    scale = queries.shape[-1] ** (-0.5)
    scores = (
        jnp.einsum("...qe,...ke->...qk", queries, keys, preferred_element_type=jnp.float32) * scale
    )
    scores = scores - jnp.max(scores, -1, keepdims=True)
    expo = jnp.exp(scores)
    weights = (expo / jnp.sum(expo, -1, keepdims=True)).astype(jnp.bfloat16)
    mixed = jnp.einsum("...qk,...ke->...qe", weights, values, preferred_element_type=jnp.float32)
    return mixed.astype(jnp.bfloat16)


def attend_items(trio):
    return attend(trio[0], trio[1], trio[2])


def general_body(
    tokens,
    cross_qkv,
    cross_out,
    depth_qkv,
    depth_out,
    up_proj,
    down_proj,
    gains,
    head_weight,
    head_bias,
):
    inlines, cross_dev, depth_dev, model_width = tokens.shape
    tok_rows = inlines * cross_dev * depth_dev
    head_count = model_width // HDIM
    cross_group = lax.axis_size("gx")
    encoding = encodings(
        inlines,
        cross_dev,
        depth_dev,
        lax.axis_index("gx") * cross_dev,
        lax.axis_index("gz") * depth_dev,
        model_width,
    )
    stream = (tokens.astype(jnp.float32) + encoding).reshape(tok_rows, model_width)
    normed = normalize(stream, gains[0])
    packed = jnp.dot(
        normed,
        lax.all_gather(cross_qkv, "gx", axis=1, tiled=True),
        preferred_element_type=jnp.float32,
    ).astype(jnp.bfloat16)
    packed = packed.reshape(inlines, cross_dev, depth_dev, 3, head_count, HDIM)
    lined = jnp.transpose(packed, (3, 0, 2, 4, 1, 5))
    per_item = inlines * depth_dev * head_count // cross_group
    lined = lined.reshape(3, cross_group, per_item, cross_dev, HDIM)
    mixed = attend_items(
        (
            lax.all_to_all(lined[0], "gx", split_axis=0, concat_axis=2, tiled=True),
            lax.all_to_all(lined[1], "gx", split_axis=0, concat_axis=2, tiled=True),
            lax.all_to_all(lined[2], "gx", split_axis=0, concat_axis=2, tiled=True),
        )
    )
    mixed = lax.all_to_all(mixed, "gx", split_axis=2, concat_axis=0, tiled=True)
    mixed = jnp.transpose(
        mixed.reshape(inlines, depth_dev, head_count, cross_dev, HDIM), (0, 3, 1, 2, 4)
    ).reshape(tok_rows, model_width)
    columns = mixed
    stream = stream + jnp.dot(
        columns,
        lax.all_gather(cross_out, "gx", axis=0, tiled=True),
        preferred_element_type=jnp.float32,
    )
    normed = normalize(stream, gains[1])
    packed = jnp.dot(
        normed,
        lax.all_gather(depth_qkv, "gx", axis=1, tiled=True),
        preferred_element_type=jnp.float32,
    ).astype(jnp.bfloat16)
    packed = packed.reshape(inlines, cross_dev, depth_dev, 3, head_count, HDIM)
    lined = jnp.transpose(packed, (3, 0, 1, 4, 2, 5))
    all_keys, all_values = (
        lax.all_gather(lined[1], "gz", axis=3, tiled=True),
        lax.all_gather(lined[2], "gz", axis=3, tiled=True),
    )
    mixed = attend(lined[0], all_keys, all_values)
    mixed = jnp.transpose(mixed, (0, 1, 3, 2, 4)).reshape(tok_rows, model_width)
    columns = mixed
    stream = stream + jnp.dot(
        columns,
        lax.all_gather(depth_out, "gx", axis=0, tiled=True),
        preferred_element_type=jnp.float32,
    )
    normed = normalize(stream, gains[2])
    hidden = jax.nn.gelu(
        jnp.dot(
            lax.all_gather(normed, "gz", axis=0, tiled=True),
            up_proj,
            preferred_element_type=jnp.float32,
        )
    ).astype(jnp.bfloat16)
    stream = stream + lax.psum_scatter(
        jnp.dot(hidden, down_proj, preferred_element_type=jnp.float32).astype(jnp.bfloat16),
        "gz",
        scatter_dimension=0,
        tiled=True,
    ).astype(jnp.float32)
    features = stream.astype(jnp.bfloat16).reshape(inlines, cross_dev, depth_dev, model_width)
    thickness = jax.nn.softplus(
        jnp.dot(stream, head_weight, precision=lax.Precision.HIGHEST) + head_bias[0]
    )
    local_time = jnp.cumsum(thickness.reshape(inlines, cross_dev, depth_dev), axis=2)
    line_total = local_time[:, :, -1]
    carried = carried_in(
        line_total, "gz", lambda earlier, later: earlier + later, jnp.zeros_like(line_total)
    )
    geotime = local_time + carried[:, :, None]
    return (features, geotime)


F32 = jnp.float32
BF16 = jnp.bfloat16
VMEM = pl.BlockSpec(memory_space=pltpu.VMEM)
SMEM = pl.BlockSpec(memory_space=pltpu.SMEM)
NT = (((1,), (1,)), ((), ()))
NEG = -1e30


def call(kernel, outs, in_specs, scratch=(), us=1, vmem=40):
    return pl.pallas_call(
        kernel,
        out_shape=outs,
        in_specs=in_specs,
        out_specs=jax.tree.map(lambda _: VMEM, outs),
        scratch_shapes=list(scratch),
        compiler_params=pltpu.CompilerParams(vmem_limit_bytes=vmem * 2**20),
        cost_estimate=pl.CostEstimate(
            flops=us * 10**9, bytes_accessed=us * 3 * 10**6, transcendentals=0
        ),
    )


class Plan:
    def __init__(self, inlines, cross_dev, depth_dev):
        self.rows = inlines * cross_dev * depth_dev
        self.cross_dev, self.depth_dev = cross_dev, depth_dev

    def inline(self, row):
        return row // (self.cross_dev * self.depth_dev)

    def depth(self, row):
        return row // self.cross_dev % self.depth_dev

    def cross(self, row):
        return row % self.cross_dev

    def column(self, row):
        return self.inline(row) * self.cross_dev + self.cross(row)

    def natural(self, row):
        return self.column(row) * self.depth_dev + self.depth(row)


def down(n, of=lambda row: row):
    return of(lax.broadcasted_iota(jnp.int32, (n, 1), 0))


def along(n, of=lambda row: row):
    return of(lax.broadcasted_iota(jnp.int32, (1, n), 1))


def one_where(mask, dtype=F32):
    return jnp.where(mask, 1.0, 0.0).astype(dtype)


def bias_where(mask):
    return jnp.where(mask, 0.0, NEG)


def rms(stream, gain):
    scale = lax.rsqrt(jnp.mean(stream * stream, -1, keepdims=True) + 1e-05)
    return (stream * scale * gain).astype(BF16)


def as_column(row):
    n = row.shape[1]
    return jnp.sum(jnp.where(down(n) == along(n), row, 0.0), axis=1, keepdims=True)


def as_row(column):
    n = column.shape[0]
    return jnp.sum(jnp.where(down(n) == along(n), column, 0.0), axis=0, keepdims=True)


def softplus(value):
    return jnp.maximum(value, 0.0) + jnp.log1p(jnp.exp(-jnp.abs(value)))


def encode_kernel(
    tokens_ref, encoding_ref, gains_ref, head_ref, stream_ref, normed_ref, out_gains_ref, out_head_ref, *, plan
):
    n = plan.rows
    to_rows = one_where(down(n, plan.natural) == along(n), BF16)
    rows = jnp.dot(to_rows, tokens_ref[...], preferred_element_type=F32)
    stream = rows + encoding_ref[...]
    stream_ref[...] = stream
    normed_ref[...] = rms(stream, gains_ref[0:1])
    out_gains_ref[...] = gains_ref[...]
    out_head_ref[...] = head_ref[...]


def attend_heads(queries, keys, values, bias, heads):
    lane = lax.broadcasted_iota(jnp.int32, (queries.shape[0], 128), 1)
    ones = jnp.ones((keys.shape[0], 128), BF16)
    outs = []
    for at in range(0, heads * HDIM, 128):
        at = slice(at, at + 128)
        wide = jnp.concatenate([values[:, at], ones], axis=1)
        pair = []
        for own in (lane < HDIM, lane >= HDIM)[: heads - at.start // HDIM]:
            masked = jnp.where(own, queries[:, at], jnp.zeros_like(queries[:, at]))
            scores = lax.dot_general(masked, keys[:, at], NT, preferred_element_type=F32) + bias
            expo = jnp.exp(scores - jnp.max(scores, -1, keepdims=True)).astype(BF16)
            mixed = jnp.dot(expo, wide, preferred_element_type=F32)
            pair.append(mixed[:, :128] / mixed[:, 128:])
        outs.append(jnp.where(lane < HDIM, pair[0], pair[-1]))
    return jnp.concatenate(outs, axis=1)


def project(normed, weights):
    return lax.dot_general(normed, weights, NT, preferred_element_type=F32).astype(BF16)


def assemble(place_ref, piece_refs, first_plane, held_ref, row, rows):
    y, c, x = place_ref[0], place_ref[1], place_ref[2]
    for n, piece_ref in enumerate(piece_refs):
        at_c = c if n < 4 else 1 - c
        flip_x, flip_y = ((0, 0), (1 - at_c, at_c), (at_c, 1 - at_c), (1, 1))[n % 4]
        at_x, at_y = x + flip_x - 2 * x * flip_x, y + flip_y - 2 * y * flip_y
        planes, _, lanes = piece_ref.shape
        at_lane = pl.multiple_of(at_x * lanes, 128)
        for plane in range(planes):
            z = place_ref[3 + first_plane + plane]
            at_row = pl.multiple_of((z * 4 + at_y * 2 + at_c) * rows, 16)
            held_ref[pl.ds(at_row, rows), pl.ds(at_lane, lanes)] = piece_ref[plane, row : row + rows]


def assemble_both(place_ref, near_refs, far_refs, held_ref, row, rows):
    assemble(place_ref, near_refs, 0, held_ref, row, rows)
    assemble(place_ref, far_refs, 2, held_ref, row, rows)


def cross_kernel(*refs, plan, rows):
    place_ref, normed_ref = refs[:2]
    piece_refs, (mixed_ref, held_ref) = refs[2:10], refs[10:]
    width = normed_ref.shape[1]
    assemble(place_ref, piece_refs, 0, held_ref, 0, rows)
    normed = normed_ref[...]
    q = project(normed, held_ref[:width]) * BF16(HDIM**-0.5)
    k = project(normed, held_ref[width : 2 * width])
    v = project(normed, held_ref[2 * width :])
    n, cross = plan.rows, plan.cross_dev
    bias = bias_where(down(n) // cross % 2 == along(n) // cross % 2)
    mixed_ref[...] = attend_heads(q, k, v, bias, width // HDIM).astype(BF16)


def cross_out_kernel(*refs, chunk, count):
    place_ref, mixed_ref, stream_ref, gains_ref = refs[:4]
    near_refs, far_refs, (out_ref, normed_ref, held_ref) = refs[4:12], refs[12:20], refs[20:]
    assemble_both(place_ref, near_refs, far_refs, held_ref, chunk, count)
    stream = stream_ref[...] + jnp.dot(mixed_ref[...], held_ref[...], preferred_element_type=F32)
    out_ref[...] = stream
    normed_ref[...] = rms(stream, gains_ref[1:2])


def depth_kernel(*refs, plan, chunk, count):
    place_ref, own_ref, peer_ref, stream_ref, gains_ref = refs[:5]
    near_refs, far_refs = refs[5:13], refs[13:21]
    out_ref, normed_ref, held_ref, out_held_ref = refs[21:]
    width = own_ref.shape[1]
    assemble_both(place_ref, near_refs, far_refs, held_ref, 0, chunk)
    assemble_both(place_ref, near_refs, far_refs, out_held_ref, chunk + count, count)
    own = own_ref[...]
    both = jnp.concatenate([own, peer_ref[...]], axis=0)
    q = project(own, held_ref[:width]) * BF16(HDIM**-0.5)
    k = project(both, held_ref[width : 2 * width])
    v = project(both, held_ref[2 * width :])
    n = plan.rows
    columns = along(2 * n, lambda row: plan.column(row % n))
    bias = bias_where(down(n, plan.column) == columns)
    mixed = attend_heads(q, k, v, bias, width // HDIM).astype(BF16)
    stream = stream_ref[...] + jnp.dot(mixed, out_held_ref[...], preferred_element_type=F32)
    out_ref[...] = stream
    normed_ref[...] = rms(stream, gains_ref[2:3])


def shift(a, step, peers):
    return lax.ppermute(a, "gx", [(i, i ^ step) for i in range(peers)])


def swap_x(a):
    return lax.ppermute(a, "gz", [(0, 1), (1, 0)])


def lane_half(shard):
    lanes = shard.shape[1] // 2
    return lax.dynamic_slice_in_dim(shard, lax.axis_index("gz") * lanes, lanes, axis=1)


def stack_kernel(*refs):
    for n, ref in enumerate(refs[:-1]):
        refs[-1][n] = ref[...]


def stack(*pieces, us=1):
    first = pieces[0]
    return call(
        stack_kernel,
        jax.ShapeDtypeStruct((len(pieces), *first.shape), first.dtype),
        [VMEM] * len(pieces),
        us=us,
        vmem=8,
    )(*pieces)


def after(value, *others):
    return lax.optimization_barrier((value, *others))[0]


def mlp_kernel(
    own_ref, peer_ref, stream_ref, up_ref, down_ref, head_ref,
    own_part_ref, peer_part_ref, own_head_ref, peer_head_ref,
):
    rows = own_ref.shape[0]
    both = jnp.concatenate([own_ref[...], peer_ref[...]], axis=0)
    hidden = jnp.dot(both, up_ref[...], preferred_element_type=F32)
    hidden = jax.nn.gelu(hidden).astype(BF16)
    part = jnp.dot(hidden, down_ref[...], preferred_element_type=F32).astype(BF16)
    own_part_ref[...] = part[:rows]
    peer_part_ref[...] = part[rows:]
    head = head_ref[...]
    own = jnp.sum((stream_ref[...] + part[:rows].astype(F32)) * head, axis=1, keepdims=True)
    peer = jnp.sum(part[rows:].astype(F32) * head, axis=1, keepdims=True)
    own_head_ref[...] = as_row(own)
    peer_head_ref[...] = as_row(peer)


def final_kernel(
    stream_ref, own_ref, got_ref, own_head_ref, got_head_ref, peer_head_ref, head_ref, bias_ref, later_ref,
    features_ref, time_ref, *, plan,
):
    n = plan.rows
    got = got_ref[...].astype(F32)
    stream = stream_ref[...] + own_ref[...].astype(F32) + got
    from_rows = one_where(down(n) == along(n, plan.natural), BF16)
    features_ref[...] = jnp.dot(
        from_rows, stream.astype(BF16), preferred_element_type=F32
    ).astype(BF16)
    bias = bias_ref[0]
    own = as_column(own_head_ref[...]) + jnp.sum(got * head_ref[...], axis=1, keepdims=True)
    own = softplus(own + bias)
    before = softplus(as_column(got_head_ref[...] + peer_head_ref[...]) + bias) * later_ref[0]
    inlines, cross_dev, depth_dev = time_ref.shape
    on_line = one_where(down(inlines * cross_dev) == along(n, plan.column))
    reached = jnp.where(down(n, plan.depth) <= along(depth_dev), own, 0.0)
    times = jnp.dot(
        on_line, reached + before, precision=lax.Precision.HIGHEST, preferred_element_type=F32
    )
    for inline in range(inlines):
        time_ref[inline] = times[inline * cross_dev : (inline + 1) * cross_dev]


def fast_body(
    tokens, cross_qkv, cross_out, depth_qkv, depth_out,
    up_proj, down_proj, gains, head_weight, head_bias,
):
    inlines, cross_dev, depth_dev, width = tokens.shape
    peers = lax.axis_size("gx")
    plan = Plan(inlines, cross_dev, depth_dev)
    rows = plan.rows
    chunk, count = cross_qkv.shape[1], cross_out.shape[0]
    shape = jax.ShapeDtypeStruct
    wide, narrow = shape((rows, width), F32), shape((rows, width), BF16)
    row = shape((1, rows), F32)

    def to(a, step, name):
        with jax.named_scope(name):
            return shift(a, step, peers)

    def to_x(a, name):
        with jax.named_scope(name):
            return swap_x(a)

    with jax.named_scope("encoding"):
        index = jnp.arange(rows)
        pairs = width // 2
        feature = jnp.arange(width)
        pair = feature // 2
        freq = math.pi * jnp.exp(-log_span * pair.astype(F32) / pairs)
        which = pair % 3
        at_cross = plan.cross(index) + lax.axis_index("gx") * cross_dev
        at_depth = plan.depth(index) + lax.axis_index("gz") * depth_dev
        position = jnp.where(
            which == 0,
            plan.inline(index)[:, None],
            jnp.where(which == 1, at_cross[:, None], at_depth[:, None]),
        )
        angle = position.astype(F32) * freq
        encoding = jnp.where(feature % 2 == 0, jnp.sin(angle), jnp.cos(angle))

    gx, x = lax.axis_index("gx"), lax.axis_index("gz")
    z, y, c = gx // 4, gx // 2 % 2, gx % 2
    planes = [z, z ^ 1, z ^ 2, z ^ 3]

    def cross_over(a, turn, name):
        pairs = []
        for device in range(2 * peers):
            of_core = device // 2 % 2
            pairs.append((device, device ^ (1 if of_core == turn else 4)))
        with jax.named_scope(name):
            return lax.ppermute(a, ("gx", "gz"), pairs)

    first_half = lane_half(cross_qkv.T)
    half = lane_half(jnp.concatenate([depth_qkv.T, cross_out, depth_out], axis=0))
    pieces = first_half, to(first_half, 4, "cross_z1"), to(first_half, 8, "cross_z2"), to(first_half, 12, "cross_z3")
    near = to(half, 4, "rest_z1")
    stream, normed, gains, head = call(
        functools.partial(encode_kernel, plan=plan),
        (wide, narrow, shape(gains.shape, F32), shape((1, width), F32)),
        [VMEM] * 4,
    )(tokens.reshape(rows, width), encoding, gains, head_weight.reshape(1, width))

    pieces, near, half, normed = lax.optimization_barrier((pieces, near, half, normed))
    far = to(half, 8, "rest_z2"), to(half, 12, "rest_z3")
    pieces = stack(*pieces)
    pieces_1, pieces_2 = cross_over(pieces, 0, "cross_1"), cross_over(pieces, 1, "cross_2")
    near = stack(half, near)
    near_1, near_2 = cross_over(near, 0, "near_1"), cross_over(near, 1, "near_2")
    lined = lax.all_to_all(
        normed.reshape(peers, rows // peers, width), "gx", split_axis=0, concat_axis=0, tiled=True
    ).reshape(rows, width)

    pieces, pieces_1, pieces_2, near, near_1, near_2, far, lined = lax.optimization_barrier(
        (pieces, pieces_1, pieces_2, near, near_1, near_2, far, lined)
    )
    pieces_3 = cross_over(pieces_1, 1, "cross_3")
    cross_pieces = [to(piece, 1, "cross_core") for piece in (pieces, pieces_1, pieces_2)]

    pieces, pieces_1, pieces_2, pieces_3, cross_pieces, near, near_1, near_2, far, lined = lax.optimization_barrier(
        (pieces, pieces_1, pieces_2, pieces_3, cross_pieces, near, near_1, near_2, far, lined)
    )
    cross_pieces = [pieces, pieces_1, pieces_2, pieces_3, *cross_pieces, to(pieces_3, 1, "cross_core")]
    near_3 = cross_over(near_1, 1, "near_3")
    far = stack(*far)
    far_1, far_2 = cross_over(far, 0, "far_1"), cross_over(far, 1, "far_2")
    near_pieces = [near, near_1, near_2, near_3]
    near_pieces += [to(piece, 1, "near_core") for piece in near_pieces]
    place = jnp.stack([y, c, x] + planes).astype(jnp.int32)
    mixed = call(
        functools.partial(cross_kernel, plan=plan, rows=chunk),
        narrow,
        [SMEM] + [VMEM] * 9,
        [pltpu.VMEM((3 * width, width), BF16)],
        us=30,
    )(place, lined, *cross_pieces)
    attended = mixed
    mixed = lax.all_to_all(
        mixed.reshape(peers, rows // peers, width), "gx", split_axis=0, concat_axis=0, tiled=True
    ).reshape(rows, width)
    far_3 = cross_over(after(far_1, far_2, attended), 1, "far_3")
    far_pieces = [far, far_1, far_2, after(far_3, mixed)]
    far_pieces += [to(piece, 1, "far_core") for piece in far_pieces]
    stream, normed = call(
        functools.partial(cross_out_kernel, chunk=chunk, count=count),
        (wide, narrow),
        [SMEM] + [VMEM] * 19,
        [pltpu.VMEM((width, width), BF16)],
        us=2,
    )(place, mixed, stream, gains, *near_pieces, *far_pieces)
    peer = to_x(normed, "normed2_x")
    stream, normed = call(
        functools.partial(depth_kernel, plan=plan, chunk=chunk, count=count),
        (wide, narrow),
        [SMEM] + [VMEM] * 20,
        [pltpu.VMEM((3 * width, width), BF16), pltpu.VMEM((width, width), BF16)],
    )(place, normed, peer, stream, gains, *near_pieces, *far_pieces)
    peer = to_x(normed, "normed3_x")
    own_part, peer_part, own_head, peer_head = call(
        mlp_kernel, (narrow, narrow, row, row), [VMEM] * 6
    )(normed, peer, stream, up_proj, down_proj, head)
    got_part, got_head = to_x(peer_part, "part_x"), to_x(own_head, "head_x")
    later = (lax.axis_index("gz") > 0).astype(F32).reshape(1)
    features, geotime = call(
        functools.partial(final_kernel, plan=plan),
        (narrow, shape(tokens.shape[:3], F32)),
        [VMEM] * 7 + [SMEM, SMEM],
    )(stream, own_part, got_part, own_head, got_head, peer_head, head, head_bias, later)
    return features.reshape(tokens.shape), geotime


def solution(mesh):
    def body(*args):
        tokens = args[0]
        inlines, cross_dev, depth_dev, width = tokens.shape
        peers = mesh.shape["gx"]
        fits = (
            (peers, mesh.shape["gz"]) == (16, 2)
            and (inlines, cross_dev, depth_dev) == (4, 4, 8)
            and width == 12 * HDIM
        )
        return (fast_body if fits else general_body)(*args)

    return jax.shard_map(
        body,
        mesh=mesh,
        in_specs=(
            P(None, "gx", "gz", None),
            P(None, "gx"),
            P("gx", None),
            P(None, "gx"),
            P("gx", None),
            P(None, "gz"),
            P("gz", None),
            P(),
            P(),
            P(),
        ),
        out_specs=(P(None, "gx", "gz", None), P(None, "gx", "gz")),
        check_vma=False,
    )
```

```python
import math
import functools

import jax
import jax.numpy as jnp
from jax import lax
from jax.experimental import pallas as pl
from jax.experimental.pallas import tpu as pltpu
from jax.sharding import PartitionSpec as P

HDIM = 64


log_span = math.log(256.0)


def carried_in(shard, axis, combine, identity):
    peers, position = (lax.axis_size(axis), lax.axis_index(axis))
    everything = lax.all_gather(shard, axis)
    start = jnp.broadcast_to(jnp.asarray(identity, shard.dtype), shard.shape)

    def step(k, before):
        reached = k < position
        new = combine(before, everything[k])
        return jnp.where(reached, new, before)

    return lax.fori_loop(0, peers, step, start)


def encodings(inlines, crosslines, depths, cross_start, depth_start, model_width):
    pairs = model_width // 2
    index = jnp.arange(pairs)
    freq = math.pi * jnp.exp(-log_span * index.astype(jnp.float32) / pairs)
    which = index % 3
    inline_pos = jnp.arange(inlines).astype(jnp.float32)[:, None, None, None]
    cross_pos = (cross_start + jnp.arange(crosslines)).astype(jnp.float32)[None, :, None, None]
    depth_pos = (depth_start + jnp.arange(depths)).astype(jnp.float32)[None, None, :, None]
    zeros = jnp.zeros((inlines, crosslines, depths, pairs), jnp.float32)
    position = jnp.where(
        which == 0, inline_pos + zeros, jnp.where(which == 1, cross_pos + zeros, depth_pos + zeros)
    )
    angle = position * freq
    return jnp.stack([jnp.sin(angle), jnp.cos(angle)], -1).reshape(
        inlines, crosslines, depths, model_width
    )


def normalize(stream, gain):
    scale = lax.rsqrt(jnp.mean(stream * stream, -1, keepdims=True) + 1e-05)
    return (stream * scale * gain).astype(jnp.bfloat16)


def attend(queries, keys, values):
    scale = queries.shape[-1] ** (-0.5)
    scores = (
        jnp.einsum("...qe,...ke->...qk", queries, keys, preferred_element_type=jnp.float32) * scale
    )
    scores = scores - jnp.max(scores, -1, keepdims=True)
    expo = jnp.exp(scores)
    weights = (expo / jnp.sum(expo, -1, keepdims=True)).astype(jnp.bfloat16)
    mixed = jnp.einsum("...qk,...ke->...qe", weights, values, preferred_element_type=jnp.float32)
    return mixed.astype(jnp.bfloat16)


def attend_items(trio):
    return attend(trio[0], trio[1], trio[2])


def general_body(
    tokens,
    cross_qkv,
    cross_out,
    depth_qkv,
    depth_out,
    up_proj,
    down_proj,
    gains,
    head_weight,
    head_bias,
):
    inlines, cross_dev, depth_dev, model_width = tokens.shape
    tok_rows = inlines * cross_dev * depth_dev
    head_count = model_width // HDIM
    cross_group = lax.axis_size("gx")
    encoding = encodings(
        inlines,
        cross_dev,
        depth_dev,
        lax.axis_index("gx") * cross_dev,
        lax.axis_index("gz") * depth_dev,
        model_width,
    )
    stream = (tokens.astype(jnp.float32) + encoding).reshape(tok_rows, model_width)
    normed = normalize(stream, gains[0])
    packed = jnp.dot(
        normed,
        lax.all_gather(cross_qkv, "gx", axis=1, tiled=True),
        preferred_element_type=jnp.float32,
    ).astype(jnp.bfloat16)
    packed = packed.reshape(inlines, cross_dev, depth_dev, 3, head_count, HDIM)
    lined = jnp.transpose(packed, (3, 0, 2, 4, 1, 5))
    per_item = inlines * depth_dev * head_count // cross_group
    lined = lined.reshape(3, cross_group, per_item, cross_dev, HDIM)
    mixed = attend_items(
        (
            lax.all_to_all(lined[0], "gx", split_axis=0, concat_axis=2, tiled=True),
            lax.all_to_all(lined[1], "gx", split_axis=0, concat_axis=2, tiled=True),
            lax.all_to_all(lined[2], "gx", split_axis=0, concat_axis=2, tiled=True),
        )
    )
    mixed = lax.all_to_all(mixed, "gx", split_axis=2, concat_axis=0, tiled=True)
    mixed = jnp.transpose(
        mixed.reshape(inlines, depth_dev, head_count, cross_dev, HDIM), (0, 3, 1, 2, 4)
    ).reshape(tok_rows, model_width)
    columns = mixed
    stream = stream + jnp.dot(
        columns,
        lax.all_gather(cross_out, "gx", axis=0, tiled=True),
        preferred_element_type=jnp.float32,
    )
    normed = normalize(stream, gains[1])
    packed = jnp.dot(
        normed,
        lax.all_gather(depth_qkv, "gx", axis=1, tiled=True),
        preferred_element_type=jnp.float32,
    ).astype(jnp.bfloat16)
    packed = packed.reshape(inlines, cross_dev, depth_dev, 3, head_count, HDIM)
    lined = jnp.transpose(packed, (3, 0, 1, 4, 2, 5))
    all_keys, all_values = (
        lax.all_gather(lined[1], "gz", axis=3, tiled=True),
        lax.all_gather(lined[2], "gz", axis=3, tiled=True),
    )
    mixed = attend(lined[0], all_keys, all_values)
    mixed = jnp.transpose(mixed, (0, 1, 3, 2, 4)).reshape(tok_rows, model_width)
    columns = mixed
    stream = stream + jnp.dot(
        columns,
        lax.all_gather(depth_out, "gx", axis=0, tiled=True),
        preferred_element_type=jnp.float32,
    )
    normed = normalize(stream, gains[2])
    hidden = jax.nn.gelu(
        jnp.dot(
            lax.all_gather(normed, "gz", axis=0, tiled=True),
            up_proj,
            preferred_element_type=jnp.float32,
        )
    ).astype(jnp.bfloat16)
    stream = stream + lax.psum_scatter(
        jnp.dot(hidden, down_proj, preferred_element_type=jnp.float32).astype(jnp.bfloat16),
        "gz",
        scatter_dimension=0,
        tiled=True,
    ).astype(jnp.float32)
    features = stream.astype(jnp.bfloat16).reshape(inlines, cross_dev, depth_dev, model_width)
    thickness = jax.nn.softplus(
        jnp.dot(stream, head_weight, precision=lax.Precision.HIGHEST) + head_bias[0]
    )
    local_time = jnp.cumsum(thickness.reshape(inlines, cross_dev, depth_dev), axis=2)
    line_total = local_time[:, :, -1]
    carried = carried_in(
        line_total, "gz", lambda earlier, later: earlier + later, jnp.zeros_like(line_total)
    )
    geotime = local_time + carried[:, :, None]
    return (features, geotime)


F32 = jnp.float32
BF16 = jnp.bfloat16
VMEM = pl.BlockSpec(memory_space=pltpu.VMEM)
SMEM = pl.BlockSpec(memory_space=pltpu.SMEM)
NT = (((1,), (1,)), ((), ()))
NEG = -1e30


def call(kernel, outs, in_specs, scratch=(), us=1, vmem=40):
    return pl.pallas_call(
        kernel,
        out_shape=outs,
        in_specs=in_specs,
        out_specs=jax.tree.map(lambda _: VMEM, outs),
        scratch_shapes=list(scratch),
        compiler_params=pltpu.CompilerParams(vmem_limit_bytes=vmem * 2**20),
        cost_estimate=pl.CostEstimate(
            flops=us * 10**9, bytes_accessed=us * 3 * 10**6, transcendentals=0
        ),
    )


class Plan:
    def __init__(self, inlines, cross_dev, depth_dev):
        self.rows = inlines * cross_dev * depth_dev
        self.cross_dev, self.depth_dev = cross_dev, depth_dev

    def inline(self, row):
        return row // (self.cross_dev * self.depth_dev)

    def depth(self, row):
        return row // self.cross_dev % self.depth_dev

    def cross(self, row):
        return row % self.cross_dev

    def column(self, row):
        return self.inline(row) * self.cross_dev + self.cross(row)

    def natural(self, row):
        return self.column(row) * self.depth_dev + self.depth(row)


def down(n, of=lambda row: row):
    return of(lax.broadcasted_iota(jnp.int32, (n, 1), 0))


def along(n, of=lambda row: row):
    return of(lax.broadcasted_iota(jnp.int32, (1, n), 1))


def one_where(mask, dtype=F32):
    return jnp.where(mask, 1.0, 0.0).astype(dtype)


def bias_where(mask):
    return jnp.where(mask, 0.0, NEG)


def rms(stream, gain):
    scale = lax.rsqrt(jnp.mean(stream * stream, -1, keepdims=True) + 1e-05)
    return (stream * scale * gain).astype(BF16)


def as_column(row):
    n = row.shape[1]
    return jnp.sum(jnp.where(down(n) == along(n), row, 0.0), axis=1, keepdims=True)


def as_row(column):
    n = column.shape[0]
    return jnp.sum(jnp.where(down(n) == along(n), column, 0.0), axis=0, keepdims=True)


def softplus(value):
    return jnp.maximum(value, 0.0) + jnp.log1p(jnp.exp(-jnp.abs(value)))


def encode_kernel(
    tokens_ref, encoding_ref, gains_ref, head_ref, stream_ref, normed_ref, out_gains_ref, out_head_ref, *, plan
):
    n = plan.rows
    to_rows = one_where(down(n, plan.natural) == along(n), BF16)
    rows = jnp.dot(to_rows, tokens_ref[...], preferred_element_type=F32)
    stream = rows + encoding_ref[...]
    stream_ref[...] = stream
    normed_ref[...] = rms(stream, gains_ref[0:1])
    out_gains_ref[...] = gains_ref[...]
    out_head_ref[...] = head_ref[...]


def attend_heads(queries, keys, values, bias, heads):
    lane = lax.broadcasted_iota(jnp.int32, (queries.shape[0], 128), 1)
    ones = jnp.ones((keys.shape[0], 128), BF16)
    outs = []
    for at in range(0, heads * HDIM, 128):
        at = slice(at, at + 128)
        wide = jnp.concatenate([values[:, at], ones], axis=1)
        pair = []
        for own in (lane < HDIM, lane >= HDIM)[: heads - at.start // HDIM]:
            masked = jnp.where(own, queries[:, at], jnp.zeros_like(queries[:, at]))
            scores = lax.dot_general(masked, keys[:, at], NT, preferred_element_type=F32) + bias
            expo = jnp.exp(scores - jnp.max(scores, -1, keepdims=True)).astype(BF16)
            mixed = jnp.dot(expo, wide, preferred_element_type=F32)
            pair.append(mixed[:, :128] / mixed[:, 128:])
        outs.append(jnp.where(lane < HDIM, pair[0], pair[-1]))
    return jnp.concatenate(outs, axis=1)


def project(normed, weights):
    return lax.dot_general(normed, weights, NT, preferred_element_type=F32).astype(BF16)


def assemble(place_ref, piece_refs, first_plane, held_ref, row, rows):
    y, c, x = place_ref[0], place_ref[1], place_ref[2]
    for n, piece_ref in enumerate(piece_refs):
        at_c = c if n < 4 else 1 - c
        flip_x, flip_y = ((0, 0), (1 - at_c, at_c), (at_c, 1 - at_c), (1, 1))[n % 4]
        at_x, at_y = x + flip_x - 2 * x * flip_x, y + flip_y - 2 * y * flip_y
        planes, _, lanes = piece_ref.shape
        at_lane = pl.multiple_of(at_x * lanes, 128)
        for plane in range(planes):
            z = place_ref[3 + first_plane + plane]
            at_row = pl.multiple_of((z * 4 + at_y * 2 + at_c) * rows, 16)
            held_ref[pl.ds(at_row, rows), pl.ds(at_lane, lanes)] = piece_ref[plane, row : row + rows]


def assemble_both(place_ref, near_refs, far_refs, held_ref, row, rows):
    assemble(place_ref, near_refs, 0, held_ref, row, rows)
    assemble(place_ref, far_refs, 2, held_ref, row, rows)


def cross_kernel(*refs, plan, rows):
    place_ref, normed_ref = refs[:2]
    piece_refs, (mixed_ref, held_ref) = refs[2:10], refs[10:]
    width = normed_ref.shape[1]
    assemble(place_ref, piece_refs, 0, held_ref, 0, rows)
    normed = normed_ref[...]
    q = project(normed, held_ref[:width]) * BF16(HDIM**-0.5)
    k = project(normed, held_ref[width : 2 * width])
    v = project(normed, held_ref[2 * width :])
    n, cross = plan.rows, plan.cross_dev
    bias = bias_where(down(n) // cross % 2 == along(n) // cross % 2)
    mixed_ref[...] = attend_heads(q, k, v, bias, width // HDIM).astype(BF16)


def cross_out_kernel(*refs, chunk, count):
    place_ref, mixed_ref, stream_ref, gains_ref = refs[:4]
    near_refs, far_refs, (out_ref, normed_ref, held_ref) = refs[4:12], refs[12:20], refs[20:]
    assemble_both(place_ref, near_refs, far_refs, held_ref, chunk, count)
    stream = stream_ref[...] + jnp.dot(mixed_ref[...], held_ref[...], preferred_element_type=F32)
    out_ref[...] = stream
    normed_ref[...] = rms(stream, gains_ref[1:2])


def depth_kernel(*refs, plan, chunk, count):
    place_ref, own_ref, peer_ref, stream_ref, gains_ref = refs[:5]
    near_refs, far_refs = refs[5:13], refs[13:21]
    out_ref, normed_ref, held_ref, out_held_ref = refs[21:]
    width = own_ref.shape[1]
    assemble_both(place_ref, near_refs, far_refs, held_ref, 0, chunk)
    assemble_both(place_ref, near_refs, far_refs, out_held_ref, chunk + count, count)
    own = own_ref[...]
    both = jnp.concatenate([own, peer_ref[...]], axis=0)
    q = project(own, held_ref[:width]) * BF16(HDIM**-0.5)
    k = project(both, held_ref[width : 2 * width])
    v = project(both, held_ref[2 * width :])
    n = plan.rows
    columns = along(2 * n, lambda row: plan.column(row % n))
    bias = bias_where(down(n, plan.column) == columns)
    mixed = attend_heads(q, k, v, bias, width // HDIM).astype(BF16)
    stream = stream_ref[...] + jnp.dot(mixed, out_held_ref[...], preferred_element_type=F32)
    out_ref[...] = stream
    normed_ref[...] = rms(stream, gains_ref[2:3])


def shift(a, step, peers):
    return lax.ppermute(a, "gx", [(i, i ^ step) for i in range(peers)])


def swap_x(a):
    return lax.ppermute(a, "gz", [(0, 1), (1, 0)])


def lane_half(shard):
    lanes = shard.shape[1] // 2
    return lax.dynamic_slice_in_dim(shard, lax.axis_index("gz") * lanes, lanes, axis=1)


def stack_kernel(*refs):
    for n, ref in enumerate(refs[:-1]):
        refs[-1][n] = ref[...]


def stack(*pieces, us=1):
    first = pieces[0]
    return call(
        stack_kernel,
        jax.ShapeDtypeStruct((len(pieces), *first.shape), first.dtype),
        [VMEM] * len(pieces),
        us=us,
        vmem=8,
    )(*pieces)


def add_kernel(first_ref, second_ref, out_ref):
    out_ref[...] = first_ref[...] + second_ref[...]


def after(value, *others):
    return lax.optimization_barrier((value, *others))[0]


def mlp_kernel(
    own_ref, peer_ref, stream_ref, up_ref, down_ref, head_ref,
    own_part_ref, peer_part_ref, own_head_ref, peer_head_ref,
):
    rows = own_ref.shape[0]
    both = jnp.concatenate([own_ref[...], peer_ref[...]], axis=0)
    hidden = jnp.dot(both, up_ref[...], preferred_element_type=F32)
    hidden = jax.nn.gelu(hidden).astype(BF16)
    part = jnp.dot(hidden, down_ref[...], preferred_element_type=F32).astype(BF16)
    own_part_ref[...] = part[:rows]
    peer_part_ref[...] = part[rows:]
    head = head_ref[...]
    own = jnp.sum((stream_ref[...] + part[:rows].astype(F32)) * head, axis=1, keepdims=True)
    peer = jnp.sum(part[rows:].astype(F32) * head, axis=1, keepdims=True)
    own_head_ref[...] = as_row(own)
    peer_head_ref[...] = as_row(peer)


def final_kernel(
    stream_ref, own_ref, got_ref, own_head_ref, got_head_ref, peer_head_ref, head_ref, bias_ref, later_ref,
    features_ref, time_ref, *, plan,
):
    n = plan.rows
    got = got_ref[...].astype(F32)
    stream = stream_ref[...] + own_ref[...].astype(F32) + got
    from_rows = one_where(down(n) == along(n, plan.natural), BF16)
    features_ref[...] = jnp.dot(
        from_rows, stream.astype(BF16), preferred_element_type=F32
    ).astype(BF16)
    bias = bias_ref[0]
    own = as_column(own_head_ref[...]) + jnp.sum(got * head_ref[...], axis=1, keepdims=True)
    own = softplus(own + bias)
    before = softplus(as_column(got_head_ref[...] + peer_head_ref[...]) + bias) * later_ref[0]
    inlines, cross_dev, depth_dev = time_ref.shape
    on_line = one_where(down(inlines * cross_dev) == along(n, plan.column))
    reached = jnp.where(down(n, plan.depth) <= along(depth_dev), own, 0.0)
    times = jnp.dot(
        on_line, reached + before, precision=lax.Precision.HIGHEST, preferred_element_type=F32
    )
    for inline in range(inlines):
        time_ref[inline] = times[inline * cross_dev : (inline + 1) * cross_dev]


def fast_body(
    tokens, cross_qkv, cross_out, depth_qkv, depth_out,
    up_proj, down_proj, gains, head_weight, head_bias,
):
    inlines, cross_dev, depth_dev, width = tokens.shape
    peers = lax.axis_size("gx")
    plan = Plan(inlines, cross_dev, depth_dev)
    rows = plan.rows
    chunk, count = cross_qkv.shape[1], cross_out.shape[0]
    shape = jax.ShapeDtypeStruct
    wide, narrow = shape((rows, width), F32), shape((rows, width), BF16)
    row = shape((1, rows), F32)

    def to(a, step, name):
        with jax.named_scope(name):
            return shift(a, step, peers)

    def to_x(a, name):
        with jax.named_scope(name):
            return swap_x(a)

    with jax.named_scope("encoding"):
        index = jnp.arange(rows)
        pairs = width // 2
        feature = jnp.arange(width)
        pair = feature // 2
        freq = math.pi * jnp.exp(-log_span * pair.astype(F32) / pairs)
        which = pair % 3
        at_cross = plan.cross(index) + lax.axis_index("gx") * cross_dev
        at_depth = plan.depth(index) + lax.axis_index("gz") * depth_dev
        position = jnp.where(
            which == 0,
            plan.inline(index)[:, None],
            jnp.where(which == 1, at_cross[:, None], at_depth[:, None]),
        )
        angle = position.astype(F32) * freq
        encoding = jnp.where(feature % 2 == 0, jnp.sin(angle), jnp.cos(angle))

    gx, x = lax.axis_index("gx"), lax.axis_index("gz")
    z, y, c = gx // 4, gx // 2 % 2, gx % 2
    planes = [z, z ^ 1, z ^ 2, z ^ 3]

    def cross_over(a, turn, name):
        pairs = []
        for device in range(2 * peers):
            of_core = device // 2 % 2
            pairs.append((device, device ^ (1 if of_core == turn else 4)))
        with jax.named_scope(name):
            return lax.ppermute(a, ("gx", "gz"), pairs)

    def diagonal(a, name):
        with jax.named_scope(name):
            return lax.ppermute(a, ("gx", "gz"), [(device, device ^ 5) for device in range(2 * peers)])

    first_half = lane_half(cross_qkv.T)
    half = lane_half(jnp.concatenate([depth_qkv.T, cross_out, depth_out], axis=0))
    pieces = first_half, to(first_half, 4, "cross_z1"), to(first_half, 8, "cross_z2"), to(first_half, 12, "cross_z3")
    near = to(half, 4, "rest_z1")
    stream, normed, gains, head = call(
        functools.partial(encode_kernel, plan=plan),
        (wide, narrow, shape(gains.shape, F32), shape((1, width), F32)),
        [VMEM] * 4,
    )(tokens.reshape(rows, width), encoding, gains, head_weight.reshape(1, width))

    pieces, near, half, normed = lax.optimization_barrier((pieces, near, half, normed))
    pieces = stack(*pieces)
    pieces_1, pieces_2 = cross_over(pieces, 0, "cross_1"), cross_over(pieces, 1, "cross_2")
    near = stack(half, near)
    with jax.named_scope("rest_middle"):
        pairs = [(4 * at + k, 12 - 4 * at + k) for at in (1, 2) for k in range(4)]
        crossed = lax.ppermute(near, "gx", pairs)
    with jax.named_scope("rest_onward"):
        pairs = [(4 * at + k, 12 * (at - 1) + k) for at in (1, 2) for k in range(4)]
        passed = lax.ppermute(crossed, "gx", pairs)
    near_1, near_2 = cross_over(near, 0, "near_1"), cross_over(near, 1, "near_2")
    lined = lax.all_to_all(
        normed.reshape(peers, rows // peers, width), "gx", split_axis=0, concat_axis=0, tiled=True
    ).reshape(rows, width)

    pieces, pieces_1, pieces_2, near, near_1, near_2, crossed, passed, lined = lax.optimization_barrier(
        (pieces, pieces_1, pieces_2, near, near_1, near_2, crossed, passed, lined)
    )
    pieces_3 = cross_over(pieces_1, 1, "cross_3")
    cross_pieces = [to(piece, 1, "cross_core") for piece in (pieces, pieces_1, pieces_2)]

    far = call(add_kernel, shape(crossed.shape, BF16), [VMEM] * 2, vmem=8)(crossed, passed)
    pieces_3, far = lax.optimization_barrier((pieces_3, far))
    cross_pieces = [pieces, pieces_1, pieces_2, pieces_3, *cross_pieces, to(pieces_3, 1, "cross_core")]
    far_1, far_2 = cross_over(far, 0, "far_1"), cross_over(far, 1, "far_2")
    inner = (z == 1) | (z == 2)
    rest_planes = [z, z ^ 1, jnp.where(inner, z ^ 3, z ^ 2), jnp.where(inner, z ^ 2, z ^ 3)]
    rest_place = jnp.stack([y, c, x] + rest_planes).astype(jnp.int32)
    place = jnp.stack([y, c, x] + planes).astype(jnp.int32)
    mixed = call(
        functools.partial(cross_kernel, plan=plan, rows=chunk),
        narrow,
        [SMEM] + [VMEM] * 9,
        [pltpu.VMEM((3 * width, width), BF16)],
        us=30,
    )(place, lined, *cross_pieces)
    mixed, far_1, near_1 = lax.optimization_barrier((mixed, far_1, near_1))
    mixed = lax.all_to_all(
        mixed.reshape(peers, rows // peers, width), "gx", split_axis=0, concat_axis=0, tiled=True
    ).reshape(rows, width)
    near_3, far_3 = cross_over(near_1, 1, "near_3"), cross_over(far_1, 1, "far_3")
    near_pieces = [near, near_1, near_2, near_3]
    near_pieces += [to(piece, 1, "near_core") for piece in near_pieces]
    far_pieces = [far, far_1, far_2, far_3]
    far_pieces += [to(piece, 1, "far_core") for piece in far_pieces]
    stream, normed = call(
        functools.partial(cross_out_kernel, chunk=chunk, count=count),
        (wide, narrow),
        [SMEM] + [VMEM] * 19,
        [pltpu.VMEM((width, width), BF16)],
        us=2,
    )(rest_place, mixed, stream, gains, *near_pieces, *far_pieces)
    peer = to_x(normed, "normed2_x")
    stream, normed = call(
        functools.partial(depth_kernel, plan=plan, chunk=chunk, count=count),
        (wide, narrow),
        [SMEM] + [VMEM] * 20,
        [pltpu.VMEM((3 * width, width), BF16), pltpu.VMEM((width, width), BF16)],
    )(rest_place, normed, peer, stream, gains, *near_pieces, *far_pieces)
    peer = to_x(normed, "normed3_x")
    own_part, peer_part, own_head, peer_head = call(
        mlp_kernel, (narrow, narrow, row, row), [VMEM] * 6
    )(normed, peer, stream, up_proj, down_proj, head)
    got_part, got_head = to_x(peer_part, "part_x"), to_x(own_head, "head_x")
    later = (lax.axis_index("gz") > 0).astype(F32).reshape(1)
    features, geotime = call(
        functools.partial(final_kernel, plan=plan),
        (narrow, shape(tokens.shape[:3], F32)),
        [VMEM] * 7 + [SMEM, SMEM],
    )(stream, own_part, got_part, own_head, got_head, peer_head, head, head_bias, later)
    return features.reshape(tokens.shape), geotime


def solution(mesh):
    def body(*args):
        tokens = args[0]
        inlines, cross_dev, depth_dev, width = tokens.shape
        peers = mesh.shape["gx"]
        fits = (
            (peers, mesh.shape["gz"]) == (16, 2)
            and (inlines, cross_dev, depth_dev) == (4, 4, 8)
            and width == 12 * HDIM
        )
        return (fast_body if fits else general_body)(*args)

    return jax.shard_map(
        body,
        mesh=mesh,
        in_specs=(
            P(None, "gx", "gz", None),
            P(None, "gx"),
            P("gx", None),
            P(None, "gx"),
            P("gx", None),
            P(None, "gz"),
            P("gz", None),
            P(),
            P(),
            P(),
        ),
        out_specs=(P(None, "gx", "gz", None), P(None, "gx", "gz")),
        check_vma=False,
    )
```

```python
import math
import functools

import jax
import jax.numpy as jnp
from jax import lax
from jax.experimental import pallas as pl
from jax.experimental.pallas import tpu as pltpu
from jax.sharding import PartitionSpec as P

HDIM = 64


log_span = math.log(256.0)


def carried_in(shard, axis, combine, identity):
    peers, position = (lax.axis_size(axis), lax.axis_index(axis))
    everything = lax.all_gather(shard, axis)
    start = jnp.broadcast_to(jnp.asarray(identity, shard.dtype), shard.shape)

    def step(k, before):
        reached = k < position
        new = combine(before, everything[k])
        return jnp.where(reached, new, before)

    return lax.fori_loop(0, peers, step, start)


def encodings(inlines, crosslines, depths, cross_start, depth_start, model_width):
    pairs = model_width // 2
    index = jnp.arange(pairs)
    freq = math.pi * jnp.exp(-log_span * index.astype(jnp.float32) / pairs)
    which = index % 3
    inline_pos = jnp.arange(inlines).astype(jnp.float32)[:, None, None, None]
    cross_pos = (cross_start + jnp.arange(crosslines)).astype(jnp.float32)[None, :, None, None]
    depth_pos = (depth_start + jnp.arange(depths)).astype(jnp.float32)[None, None, :, None]
    zeros = jnp.zeros((inlines, crosslines, depths, pairs), jnp.float32)
    position = jnp.where(
        which == 0, inline_pos + zeros, jnp.where(which == 1, cross_pos + zeros, depth_pos + zeros)
    )
    angle = position * freq
    return jnp.stack([jnp.sin(angle), jnp.cos(angle)], -1).reshape(
        inlines, crosslines, depths, model_width
    )


def normalize(stream, gain):
    scale = lax.rsqrt(jnp.mean(stream * stream, -1, keepdims=True) + 1e-05)
    return (stream * scale * gain).astype(jnp.bfloat16)


def attend(queries, keys, values):
    scale = queries.shape[-1] ** (-0.5)
    scores = (
        jnp.einsum("...qe,...ke->...qk", queries, keys, preferred_element_type=jnp.float32) * scale
    )
    scores = scores - jnp.max(scores, -1, keepdims=True)
    expo = jnp.exp(scores)
    weights = (expo / jnp.sum(expo, -1, keepdims=True)).astype(jnp.bfloat16)
    mixed = jnp.einsum("...qk,...ke->...qe", weights, values, preferred_element_type=jnp.float32)
    return mixed.astype(jnp.bfloat16)


def attend_items(trio):
    return attend(trio[0], trio[1], trio[2])


def general_body(
    tokens,
    cross_qkv,
    cross_out,
    depth_qkv,
    depth_out,
    up_proj,
    down_proj,
    gains,
    head_weight,
    head_bias,
):
    inlines, cross_dev, depth_dev, model_width = tokens.shape
    tok_rows = inlines * cross_dev * depth_dev
    head_count = model_width // HDIM
    cross_group = lax.axis_size("gx")
    encoding = encodings(
        inlines,
        cross_dev,
        depth_dev,
        lax.axis_index("gx") * cross_dev,
        lax.axis_index("gz") * depth_dev,
        model_width,
    )
    stream = (tokens.astype(jnp.float32) + encoding).reshape(tok_rows, model_width)
    normed = normalize(stream, gains[0])
    packed = jnp.dot(
        normed,
        lax.all_gather(cross_qkv, "gx", axis=1, tiled=True),
        preferred_element_type=jnp.float32,
    ).astype(jnp.bfloat16)
    packed = packed.reshape(inlines, cross_dev, depth_dev, 3, head_count, HDIM)
    lined = jnp.transpose(packed, (3, 0, 2, 4, 1, 5))
    per_item = inlines * depth_dev * head_count // cross_group
    lined = lined.reshape(3, cross_group, per_item, cross_dev, HDIM)
    mixed = attend_items(
        (
            lax.all_to_all(lined[0], "gx", split_axis=0, concat_axis=2, tiled=True),
            lax.all_to_all(lined[1], "gx", split_axis=0, concat_axis=2, tiled=True),
            lax.all_to_all(lined[2], "gx", split_axis=0, concat_axis=2, tiled=True),
        )
    )
    mixed = lax.all_to_all(mixed, "gx", split_axis=2, concat_axis=0, tiled=True)
    mixed = jnp.transpose(
        mixed.reshape(inlines, depth_dev, head_count, cross_dev, HDIM), (0, 3, 1, 2, 4)
    ).reshape(tok_rows, model_width)
    columns = mixed
    stream = stream + jnp.dot(
        columns,
        lax.all_gather(cross_out, "gx", axis=0, tiled=True),
        preferred_element_type=jnp.float32,
    )
    normed = normalize(stream, gains[1])
    packed = jnp.dot(
        normed,
        lax.all_gather(depth_qkv, "gx", axis=1, tiled=True),
        preferred_element_type=jnp.float32,
    ).astype(jnp.bfloat16)
    packed = packed.reshape(inlines, cross_dev, depth_dev, 3, head_count, HDIM)
    lined = jnp.transpose(packed, (3, 0, 1, 4, 2, 5))
    all_keys, all_values = (
        lax.all_gather(lined[1], "gz", axis=3, tiled=True),
        lax.all_gather(lined[2], "gz", axis=3, tiled=True),
    )
    mixed = attend(lined[0], all_keys, all_values)
    mixed = jnp.transpose(mixed, (0, 1, 3, 2, 4)).reshape(tok_rows, model_width)
    columns = mixed
    stream = stream + jnp.dot(
        columns,
        lax.all_gather(depth_out, "gx", axis=0, tiled=True),
        preferred_element_type=jnp.float32,
    )
    normed = normalize(stream, gains[2])
    hidden = jax.nn.gelu(
        jnp.dot(
            lax.all_gather(normed, "gz", axis=0, tiled=True),
            up_proj,
            preferred_element_type=jnp.float32,
        )
    ).astype(jnp.bfloat16)
    stream = stream + lax.psum_scatter(
        jnp.dot(hidden, down_proj, preferred_element_type=jnp.float32).astype(jnp.bfloat16),
        "gz",
        scatter_dimension=0,
        tiled=True,
    ).astype(jnp.float32)
    features = stream.astype(jnp.bfloat16).reshape(inlines, cross_dev, depth_dev, model_width)
    thickness = jax.nn.softplus(
        jnp.dot(stream, head_weight, precision=lax.Precision.HIGHEST) + head_bias[0]
    )
    local_time = jnp.cumsum(thickness.reshape(inlines, cross_dev, depth_dev), axis=2)
    line_total = local_time[:, :, -1]
    carried = carried_in(
        line_total, "gz", lambda earlier, later: earlier + later, jnp.zeros_like(line_total)
    )
    geotime = local_time + carried[:, :, None]
    return (features, geotime)


F32 = jnp.float32
BF16 = jnp.bfloat16
VMEM = pl.BlockSpec(memory_space=pltpu.VMEM)
SMEM = pl.BlockSpec(memory_space=pltpu.SMEM)
NT = (((1,), (1,)), ((), ()))
NEG = -1e30


def call(kernel, outs, in_specs, scratch=(), us=1, vmem=40):
    return pl.pallas_call(
        kernel,
        out_shape=outs,
        in_specs=in_specs,
        out_specs=jax.tree.map(lambda _: VMEM, outs),
        scratch_shapes=list(scratch),
        compiler_params=pltpu.CompilerParams(vmem_limit_bytes=vmem * 2**20),
        cost_estimate=pl.CostEstimate(
            flops=us * 10**9, bytes_accessed=us * 3 * 10**6, transcendentals=0
        ),
    )


class Plan:
    def __init__(self, inlines, cross_dev, depth_dev):
        self.rows = inlines * cross_dev * depth_dev
        self.cross_dev, self.depth_dev = cross_dev, depth_dev

    def inline(self, row):
        return row // (self.cross_dev * self.depth_dev)

    def depth(self, row):
        return row // self.cross_dev % self.depth_dev

    def cross(self, row):
        return row % self.cross_dev

    def column(self, row):
        return self.inline(row) * self.cross_dev + self.cross(row)

    def natural(self, row):
        return self.column(row) * self.depth_dev + self.depth(row)


def down(n, of=lambda row: row):
    return of(lax.broadcasted_iota(jnp.int32, (n, 1), 0))


def along(n, of=lambda row: row):
    return of(lax.broadcasted_iota(jnp.int32, (1, n), 1))


def one_where(mask, dtype=F32):
    return jnp.where(mask, 1.0, 0.0).astype(dtype)


def bias_where(mask):
    return jnp.where(mask, 0.0, NEG)


def rms(stream, gain):
    scale = lax.rsqrt(jnp.mean(stream * stream, -1, keepdims=True) + 1e-05)
    return (stream * scale * gain).astype(BF16)


def as_column(row):
    n = row.shape[1]
    return jnp.sum(jnp.where(down(n) == along(n), row, 0.0), axis=1, keepdims=True)


def as_row(column):
    n = column.shape[0]
    return jnp.sum(jnp.where(down(n) == along(n), column, 0.0), axis=0, keepdims=True)


def softplus(value):
    return jnp.maximum(value, 0.0) + jnp.log1p(jnp.exp(-jnp.abs(value)))


def encode_kernel(
    tokens_ref, encoding_ref, gains_ref, head_ref, stream_ref, normed_ref, out_gains_ref, out_head_ref, *, plan
):
    n = plan.rows
    to_rows = one_where(down(n, plan.natural) == along(n), BF16)
    rows = jnp.dot(to_rows, tokens_ref[...], preferred_element_type=F32)
    stream = rows + encoding_ref[...]
    stream_ref[...] = stream
    normed_ref[...] = rms(stream, gains_ref[0:1])
    out_gains_ref[...] = gains_ref[...]
    out_head_ref[...] = head_ref[...]


def attend_heads(queries, keys, values, bias, heads):
    lane = lax.broadcasted_iota(jnp.int32, (queries.shape[0], 128), 1)
    ones = jnp.ones((keys.shape[0], 128), BF16)
    outs = []
    for at in range(0, heads * HDIM, 128):
        at = slice(at, at + 128)
        wide = jnp.concatenate([values[:, at], ones], axis=1)
        pair = []
        for own in (lane < HDIM, lane >= HDIM)[: heads - at.start // HDIM]:
            masked = jnp.where(own, queries[:, at], jnp.zeros_like(queries[:, at]))
            scores = lax.dot_general(masked, keys[:, at], NT, preferred_element_type=F32) + bias
            expo = jnp.exp(scores - jnp.max(scores, -1, keepdims=True)).astype(BF16)
            mixed = jnp.dot(expo, wide, preferred_element_type=F32)
            pair.append(mixed[:, :128] / mixed[:, 128:])
        outs.append(jnp.where(lane < HDIM, pair[0], pair[-1]))
    return jnp.concatenate(outs, axis=1)


def project(normed, weights):
    return lax.dot_general(normed, weights, NT, preferred_element_type=F32).astype(BF16)


def assemble(place_ref, piece_refs, first_plane, held_ref, row, rows):
    y, c, x = place_ref[0], place_ref[1], place_ref[2]
    for n, piece_ref in enumerate(piece_refs):
        at_c = c if n < 4 else 1 - c
        flip_x, flip_y = ((0, 0), (1 - at_c, at_c), (at_c, 1 - at_c), (1, 1))[n % 4]
        at_x, at_y = x + flip_x - 2 * x * flip_x, y + flip_y - 2 * y * flip_y
        planes, _, lanes = piece_ref.shape
        at_lane = pl.multiple_of(at_x * lanes, 128)
        for plane in range(planes):
            z = place_ref[3 + first_plane + plane]
            at_row = pl.multiple_of((z * 4 + at_y * 2 + at_c) * rows, 16)
            held_ref[pl.ds(at_row, rows), pl.ds(at_lane, lanes)] = piece_ref[plane, row : row + rows]


def assemble_both(place_ref, near_refs, far_refs, held_ref, row, rows):
    assemble(place_ref, near_refs, 0, held_ref, row, rows)
    assemble(place_ref, far_refs, 2, held_ref, row, rows)


def cross_kernel(*refs, plan, rows):
    place_ref, normed_ref = refs[:2]
    piece_refs, (mixed_ref, held_ref) = refs[2:10], refs[10:]
    width = normed_ref.shape[1]
    assemble(place_ref, piece_refs, 0, held_ref, 0, rows)
    normed = normed_ref[...]
    q = project(normed, held_ref[:width]) * BF16(HDIM**-0.5)
    k = project(normed, held_ref[width : 2 * width])
    v = project(normed, held_ref[2 * width :])
    n, cross = plan.rows, plan.cross_dev
    bias = bias_where(down(n) // cross % 2 == along(n) // cross % 2)
    mixed_ref[...] = attend_heads(q, k, v, bias, width // HDIM).astype(BF16)


def cross_out_kernel(*refs, chunk, count):
    place_ref, mixed_ref, stream_ref, gains_ref = refs[:4]
    near_refs, far_refs, (out_ref, normed_ref, held_ref) = refs[4:12], refs[12:20], refs[20:]
    assemble_both(place_ref, near_refs, far_refs, held_ref, chunk, count)
    stream = stream_ref[...] + jnp.dot(mixed_ref[...], held_ref[...], preferred_element_type=F32)
    out_ref[...] = stream
    normed_ref[...] = rms(stream, gains_ref[1:2])


def depth_own_kernel(*refs, chunk, count):
    place_ref, own_ref = refs[:2]
    near_refs, far_refs, (q_ref, kv_ref, held_ref, out_held_ref) = refs[2:10], refs[10:18], refs[18:]
    width = own_ref.shape[1]
    assemble_both(place_ref, near_refs, far_refs, held_ref, 0, chunk)
    assemble_both(place_ref, near_refs, far_refs, out_held_ref, chunk + count, count)
    own = own_ref[...]
    q_ref[...] = project(own, held_ref[:width]) * BF16(HDIM**-0.5)
    kv_ref[...] = project(own, held_ref[width:])


def depth_kernel(
    peer_ref, stream_ref, gains_ref, q_ref, kv_ref, held_ref, out_held_ref, out_ref, normed_ref, *, plan
):
    width = peer_ref.shape[1]
    kv = jnp.concatenate([kv_ref[...], project(peer_ref[...], held_ref[width:])], axis=0)
    n = plan.rows
    columns = along(2 * n, lambda row: plan.column(row % n))
    bias = bias_where(down(n, plan.column) == columns)
    mixed = attend_heads(q_ref[...], kv[:, :width], kv[:, width:], bias, width // HDIM).astype(BF16)
    stream = stream_ref[...] + jnp.dot(mixed, out_held_ref[...], preferred_element_type=F32)
    out_ref[...] = stream
    normed_ref[...] = rms(stream, gains_ref[2:3])


def shift(a, step, peers):
    return lax.ppermute(a, "gx", [(i, i ^ step) for i in range(peers)])


def swap_x(a):
    return lax.ppermute(a, "gz", [(0, 1), (1, 0)])


def lane_half(shard):
    lanes = shard.shape[1] // 2
    return lax.dynamic_slice_in_dim(shard, lax.axis_index("gz") * lanes, lanes, axis=1)


def stack_kernel(*refs):
    for n, ref in enumerate(refs[:-1]):
        refs[-1][n] = ref[...]


def stack(*pieces, us=1):
    first = pieces[0]
    return call(
        stack_kernel,
        jax.ShapeDtypeStruct((len(pieces), *first.shape), first.dtype),
        [VMEM] * len(pieces),
        us=us,
        vmem=8,
    )(*pieces)


def add_kernel(first_ref, second_ref, out_ref):
    out_ref[...] = first_ref[...] + second_ref[...]


def after(value, *others):
    return lax.optimization_barrier((value, *others))[0]


def mlp_kernel(
    own_ref, peer_ref, stream_ref, up_ref, down_ref, head_ref,
    own_part_ref, peer_part_ref, own_head_ref, peer_head_ref,
):
    rows = own_ref.shape[0]
    both = jnp.concatenate([own_ref[...], peer_ref[...]], axis=0)
    hidden = jnp.dot(both, up_ref[...], preferred_element_type=F32)
    hidden = jax.nn.gelu(hidden).astype(BF16)
    part = jnp.dot(hidden, down_ref[...], preferred_element_type=F32).astype(BF16)
    own_part_ref[...] = part[:rows]
    peer_part_ref[...] = part[rows:]
    head = head_ref[...]
    own = jnp.sum((stream_ref[...] + part[:rows].astype(F32)) * head, axis=1, keepdims=True)
    peer = jnp.sum(part[rows:].astype(F32) * head, axis=1, keepdims=True)
    own_head_ref[...] = as_row(own)
    peer_head_ref[...] = as_row(peer)


def final_kernel(
    stream_ref, own_ref, got_ref, own_head_ref, got_head_ref, peer_head_ref, head_ref, bias_ref, later_ref,
    features_ref, time_ref, *, plan,
):
    n = plan.rows
    got = got_ref[...].astype(F32)
    stream = stream_ref[...] + own_ref[...].astype(F32) + got
    from_rows = one_where(down(n) == along(n, plan.natural), BF16)
    features_ref[...] = jnp.dot(
        from_rows, stream.astype(BF16), preferred_element_type=F32
    ).astype(BF16)
    bias = bias_ref[0]
    own = as_column(own_head_ref[...]) + jnp.sum(got * head_ref[...], axis=1, keepdims=True)
    own = softplus(own + bias)
    before = softplus(as_column(got_head_ref[...] + peer_head_ref[...]) + bias) * later_ref[0]
    inlines, cross_dev, depth_dev = time_ref.shape
    on_line = one_where(down(inlines * cross_dev) == along(n, plan.column))
    reached = jnp.where(down(n, plan.depth) <= along(depth_dev), own, 0.0)
    times = jnp.dot(
        on_line, reached + before, precision=lax.Precision.HIGHEST, preferred_element_type=F32
    )
    for inline in range(inlines):
        time_ref[inline] = times[inline * cross_dev : (inline + 1) * cross_dev]


def fast_body(
    tokens, cross_qkv, cross_out, depth_qkv, depth_out,
    up_proj, down_proj, gains, head_weight, head_bias,
):
    inlines, cross_dev, depth_dev, width = tokens.shape
    peers = lax.axis_size("gx")
    plan = Plan(inlines, cross_dev, depth_dev)
    rows = plan.rows
    chunk, count = cross_qkv.shape[1], cross_out.shape[0]
    shape = jax.ShapeDtypeStruct
    wide, narrow = shape((rows, width), F32), shape((rows, width), BF16)
    row = shape((1, rows), F32)

    def to(a, step, name):
        with jax.named_scope(name):
            return shift(a, step, peers)

    def to_x(a, name):
        with jax.named_scope(name):
            return swap_x(a)

    with jax.named_scope("encoding"):
        index = jnp.arange(rows)
        pairs = width // 2
        feature = jnp.arange(width)
        pair = feature // 2
        freq = math.pi * jnp.exp(-log_span * pair.astype(F32) / pairs)
        which = pair % 3
        at_cross = plan.cross(index) + lax.axis_index("gx") * cross_dev
        at_depth = plan.depth(index) + lax.axis_index("gz") * depth_dev
        position = jnp.where(
            which == 0,
            plan.inline(index)[:, None],
            jnp.where(which == 1, at_cross[:, None], at_depth[:, None]),
        )
        angle = position.astype(F32) * freq
        encoding = jnp.where(feature % 2 == 0, jnp.sin(angle), jnp.cos(angle))

    gx, x = lax.axis_index("gx"), lax.axis_index("gz")
    z, y, c = gx // 4, gx // 2 % 2, gx % 2
    planes = [z, z ^ 1, z ^ 2, z ^ 3]

    def cross_over(a, turn, name):
        pairs = []
        for device in range(2 * peers):
            of_core = device // 2 % 2
            pairs.append((device, device ^ (1 if of_core == turn else 4)))
        with jax.named_scope(name):
            return lax.ppermute(a, ("gx", "gz"), pairs)

    def diagonal(a, name):
        with jax.named_scope(name):
            return lax.ppermute(a, ("gx", "gz"), [(device, device ^ 5) for device in range(2 * peers)])

    first_half = lane_half(cross_qkv.T)
    half = lane_half(jnp.concatenate([depth_qkv.T, cross_out, depth_out], axis=0))
    pieces = first_half, to(first_half, 4, "cross_z1"), to(first_half, 8, "cross_z2"), to(first_half, 12, "cross_z3")
    near = to(half, 4, "rest_z1")
    stream, normed, gains, head = call(
        functools.partial(encode_kernel, plan=plan),
        (wide, narrow, shape(gains.shape, F32), shape((1, width), F32)),
        [VMEM] * 4,
    )(tokens.reshape(rows, width), encoding, gains, head_weight.reshape(1, width))

    pieces, near, half, normed = lax.optimization_barrier((pieces, near, half, normed))
    pieces = stack(*pieces)
    pieces_1, pieces_2 = cross_over(pieces, 0, "cross_1"), cross_over(pieces, 1, "cross_2")
    near = stack(half, near)
    with jax.named_scope("rest_middle"):
        pairs = [(4 * at + k, 12 - 4 * at + k) for at in (1, 2) for k in range(4)]
        crossed = lax.ppermute(near, "gx", pairs)
    with jax.named_scope("rest_onward"):
        pairs = [(4 * at + k, 12 * (at - 1) + k) for at in (1, 2) for k in range(4)]
        passed = lax.ppermute(crossed, "gx", pairs)
    near_1, near_2 = cross_over(near, 0, "near_1"), cross_over(near, 1, "near_2")
    lined = lax.all_to_all(
        normed.reshape(peers, rows // peers, width), "gx", split_axis=0, concat_axis=0, tiled=True
    ).reshape(rows, width)

    pieces, pieces_1, pieces_2, near, near_1, near_2, crossed, passed, lined = lax.optimization_barrier(
        (pieces, pieces_1, pieces_2, near, near_1, near_2, crossed, passed, lined)
    )
    pieces_3 = cross_over(pieces_1, 1, "cross_3")
    cross_pieces = [to(piece, 1, "cross_core") for piece in (pieces, pieces_1, pieces_2)]

    far = call(add_kernel, shape(crossed.shape, BF16), [VMEM] * 2, vmem=8)(crossed, passed)
    pieces_3, far = lax.optimization_barrier((pieces_3, far))
    cross_pieces = [pieces, pieces_1, pieces_2, pieces_3, *cross_pieces, to(pieces_3, 1, "cross_core")]
    far_1, far_2 = cross_over(far, 0, "far_1"), cross_over(far, 1, "far_2")
    inner = (z == 1) | (z == 2)
    rest_planes = [z, z ^ 1, jnp.where(inner, z ^ 3, z ^ 2), jnp.where(inner, z ^ 2, z ^ 3)]
    rest_place = jnp.stack([y, c, x] + rest_planes).astype(jnp.int32)
    place = jnp.stack([y, c, x] + planes).astype(jnp.int32)
    mixed = call(
        functools.partial(cross_kernel, plan=plan, rows=chunk),
        narrow,
        [SMEM] + [VMEM] * 9,
        [pltpu.VMEM((3 * width, width), BF16)],
        us=30,
    )(place, lined, *cross_pieces)
    mixed, far_1, near_1 = lax.optimization_barrier((mixed, far_1, near_1))
    mixed = lax.all_to_all(
        mixed.reshape(peers, rows // peers, width), "gx", split_axis=0, concat_axis=0, tiled=True
    ).reshape(rows, width)
    near_3, far_3 = cross_over(near_1, 1, "near_3"), cross_over(far_1, 1, "far_3")
    near_pieces = [near, near_1, near_2, near_3]
    near_pieces += [to(piece, 1, "near_core") for piece in near_pieces]
    far_pieces = [far, far_1, far_2, far_3]
    far_pieces += [to(piece, 1, "far_core") for piece in far_pieces]
    stream, normed = call(
        functools.partial(cross_out_kernel, chunk=chunk, count=count),
        (wide, narrow),
        [SMEM] + [VMEM] * 19,
        [pltpu.VMEM((width, width), BF16)],
        us=2,
    )(rest_place, mixed, stream, gains, *near_pieces, *far_pieces)
    peer = to_x(normed, "normed2_x")
    own_side = call(
        functools.partial(depth_own_kernel, chunk=chunk, count=count),
        (narrow, shape((rows, 2 * width), BF16), shape((3 * width, width), BF16), shape((width, width), BF16)),
        [SMEM] + [VMEM] * 17,
        us=5,
    )(rest_place, normed, *near_pieces, *far_pieces)
    stream, normed = call(
        functools.partial(depth_kernel, plan=plan), (wide, narrow), [VMEM] * 7, us=3
    )(peer, stream, gains, *own_side)
    peer = to_x(normed, "normed3_x")
    own_part, peer_part, own_head, peer_head = call(
        mlp_kernel, (narrow, narrow, row, row), [VMEM] * 6
    )(normed, peer, stream, up_proj, down_proj, head)
    got_part, got_head = to_x(peer_part, "part_x"), to_x(own_head, "head_x")
    later = (lax.axis_index("gz") > 0).astype(F32).reshape(1)
    features, geotime = call(
        functools.partial(final_kernel, plan=plan),
        (narrow, shape(tokens.shape[:3], F32)),
        [VMEM] * 7 + [SMEM, SMEM],
    )(stream, own_part, got_part, own_head, got_head, peer_head, head, head_bias, later)
    return features.reshape(tokens.shape), geotime


def solution(mesh):
    def body(*args):
        tokens = args[0]
        inlines, cross_dev, depth_dev, width = tokens.shape
        peers = mesh.shape["gx"]
        fits = (
            (peers, mesh.shape["gz"]) == (16, 2)
            and (inlines, cross_dev, depth_dev) == (4, 4, 8)
            and width == 12 * HDIM
        )
        return (fast_body if fits else general_body)(*args)

    return jax.shard_map(
        body,
        mesh=mesh,
        in_specs=(
            P(None, "gx", "gz", None),
            P(None, "gx"),
            P("gx", None),
            P(None, "gx"),
            P("gx", None),
            P(None, "gz"),
            P("gz", None),
            P(),
            P(),
            P(),
        ),
        out_specs=(P(None, "gx", "gz", None), P(None, "gx", "gz")),
        check_vma=False,
    )
```
